128 devices in a mesh: sect: 8 (over x, core), cell: 16 (over y, z).
Axes of the slice: x: 4, y: 4, z: 4, core: 2. Of those that a mesh axis runs over, the one named last changes fastest.
Arguments:
- atm_fields: bfloat16 [24, 524288], P(None, ('sect', 'cell')), may hold values from -6 to 6
- ocn_state: float32 [8, 1048576], P(None, ('sect', 'cell')), may hold values from -6 to 6
- ice_state: float32 [8, 1048576], P(None, ('sect', 'cell')), may hold values from -6 to 6
- ice_level: int32 [1048576], P(('sect', 'cell')), may hold values from 0 to 8
- lnd_state: float32 [8, 262144], P(None, ('sect', 'cell')), may hold values from -6 to 6
- lnd_level: int32 [262144], P(('sect', 'cell')), may hold values from 1 to 8
- ocn_map: int32 [8192, 2], P(('sect', 'cell')), may hold values from 0 to 4095, as said below
- ocn_local: int32 [8192, 2], P(('sect', 'cell')), may hold values from 0 to 31
- ocn_tiles: bfloat16 [8192, 4, 128, 128], P(('sect', 'cell')), may hold values from -0.25 to 0.25
- lnd_map: int32 [2048, 2], P(('sect', 'cell')), may hold values from 0 to 4095, as said below
- lnd_local: int32 [2048, 2], P(('sect', 'cell')), may hold values from 0 to 31
- lnd_tiles: bfloat16 [2048, 4, 128, 128], P(('sect', 'cell')), may hold values from -0.25 to 0.25
Outputs:
- atm_flux: float32 [8, 524288], P(None, ('sect', 'cell'))
- ocn_flux: float32 [8, 1048576], P(None, ('sect', 'cell'))
- lnd_flux: float32 [8, 262144], P(None, ('sect', 'cell'))
The draws below stay inside these ranges and needn't reach their ends.
Inputs may be any that keep to these rules, and one draw needn't show every extreme that they name: Global atmosphere block indices; the device of block b is b // 32, and devices are numbered sect-major. For the ocn_map rows of one device q's 64 ocean blocks taken together with the lnd_map rows of its 16 land blocks, every named device is (q + t) modulo the device count for some t from -8 to 7; at most 15 of these entries name any one device, and exactly 15 name some device. `lnd_map`: global atmosphere block indices, counted together with ocn_map as stated there.
All inputs are finite; a program needn't handle non-finite values.
Results may differ from the reference program's by a relative error of at most 0.0022.
Values may be sent and summed in bfloat16 or wider, within the bound.
No kernel may reach another device: no remote copies, remote signals or barrier semaphores. Data moves between devices by JAX's collectives and lax.ppermute only.
A program may use at most 64 MiB of HBM per device.

```python
import jax
import jax.numpy as jnp
from jax import lax

FIELDS = 24
FLUXES = 8
BLOCK = 128
KR = 2
KL = 2
AB_DEV = 32
OB_DEV = 64
LB_DEV = 16
C_PEER = 15
NAB = 4096
NA = 524288
NOB = 8192
NO = 1048576
NLB = 2048
NL = 262144
N_SECT = 8
N_CELL = 16


def remote_sources(key):
    key = jax.random.fold_in(key, 7)
    device_count = NAB // AB_DEV
    pair_count = (OB_DEV + LB_DEV) * KR
    window = N_CELL
    offsets = jnp.arange(window, dtype=jnp.int32) - window // 2
    copies = window * C_PEER

    def draw_device(subkey, device):
        key_heavy, key_score, key_order, key_local = jax.random.split(subkey, 4)
        heavy = jax.random.randint(key_heavy, (), 0, window).astype(jnp.int32)
        peer = jnp.repeat(jnp.arange(window, dtype=jnp.int32), C_PEER)
        noise = jax.random.randint(key_score, (copies,), 0, 3 * window).astype(jnp.int32)
        score = noise + 2 * jnp.abs(offsets[peer])
        score = jnp.where(peer == heavy, -1, score)
        keyed = (score + 1) * copies + jnp.arange(copies, dtype=jnp.int32)
        chosen = peer[jnp.argsort(keyed)[:pair_count]]
        owners = (device + offsets[chosen]) % device_count
        owners = jax.random.permutation(key_order, owners).astype(jnp.int32)
        local_block = jax.random.randint(key_local, (pair_count,), 0, AB_DEV).astype(jnp.int32)
        return (owners * AB_DEV + local_block).astype(jnp.int32)
    keys = jax.random.split(key, device_count)
    return jax.vmap(draw_device)(keys, jnp.arange(device_count, dtype=jnp.int32))


def draw_ocn_map(key, part):
    source_table = remote_sources(key)
    return source_table[:, :OB_DEV * KR].reshape(-1, KR)


def draw_lnd_map(key, part):
    source_table = remote_sources(key)
    return source_table[:, OB_DEV * KR:].reshape(-1, KR)


def set_ends(entries, rng, least, top_value):
    index_at = [jax.random.randint(jax.random.fold_in(rng, axis), (), 0, length) for axis, length in enumerate(entries.shape)]
    main_axis = entries.shape.index(max(entries.shape))
    next_to = index_at[:main_axis] + [(index_at[main_axis] + 1) % entries.shape[main_axis]] + index_at[main_axis + 1:]
    return entries.at[tuple(index_at)].set(least).at[tuple(next_to)].set(top_value)


def block_levels(key, dims, shards, low, top_value):
    def one(dim, shards_of):
        steps = jax.random.uniform(jax.random.fold_in(jax.random.fold_in(key, 6), dim), (shards_of,), jnp.float32, low / len(shards), top_value / len(shards))
        return jnp.repeat(jnp.exp(steps), dims[dim] // shards_of).reshape((-1,) + (1,) * (len(dims) - dim - 1))

    factor_of = one(*shards[0])
    for cut in shards[1:]:
        factor_of = factor_of * one(*cut)
    return factor_of


def normal_values(stream_key, extent, width, most, cuts=(), kind=jnp.bfloat16):
    drawn = width * jax.random.normal(stream_key, extent, jnp.float32)
    if cuts:
        drawn = drawn * block_levels(stream_key, extent, cuts, -0.22, 0.18)
    return jnp.clip(drawn, -most, most).astype(kind)


def setup_inputs(seed: int = 0) -> dict:
    seeds = jax.random.split(jax.random.key(seed), 13)
    atm_fields = normal_values(seeds[0], (FIELDS, NA), 1.0, 6.0, ((1, 128),))
    ocn_state = normal_values(seeds[1], (FLUXES, NO), 1.0, 6.0, ((1, 128),), jnp.float32)
    ice_state = normal_values(seeds[2], (FLUXES, NO), 1.0, 6.0, ((1, 128),), jnp.float32)
    ice_level = set_ends(jax.random.randint(seeds[3], (NO,), 0, 9), jax.random.fold_in(seeds[3], 1), 0, 8).astype(jnp.int32)
    lnd_state = normal_values(seeds[4], (FLUXES, NL), 1.0, 6.0, ((1, 128),), jnp.float32)
    lnd_level = set_ends(jax.random.randint(seeds[5], (NL,), 1, 9), jax.random.fold_in(seeds[5], 1), 1, 8).astype(jnp.int32)
    ocn_map = draw_ocn_map(jax.random.fold_in(seeds[12], 71), 0)
    ocn_local = set_ends(jax.random.randint(seeds[7], (NOB, KL), 0, AB_DEV), jax.random.fold_in(seeds[7], 1), 0, AB_DEV - 1).astype(jnp.int32)
    ocn_tiles = normal_values(seeds[8], (NOB, KR + KL, BLOCK, BLOCK), (BLOCK * (KR + KL)) ** -0.5, 0.25, ((0, 128),))
    lnd_map = draw_lnd_map(jax.random.fold_in(seeds[12], 71), 0)
    lnd_local = set_ends(jax.random.randint(seeds[10], (NLB, KL), 0, AB_DEV), jax.random.fold_in(seeds[10], 1), 0, AB_DEV - 1).astype(jnp.int32)
    lnd_tiles = normal_values(seeds[11], (NLB, KR + KL, BLOCK, BLOCK), (BLOCK * (KR + KL)) ** -0.5, 0.25, ((0, 128),))
    return {"atm_fields": atm_fields, "ocn_state": ocn_state, "ice_state": ice_state, "ice_level": ice_level, "lnd_state": lnd_state, "lnd_level": lnd_level, "ocn_map": ocn_map, "ocn_local": ocn_local, "ocn_tiles": ocn_tiles, "lnd_map": lnd_map, "lnd_local": lnd_local, "lnd_tiles": lnd_tiles}


ocean_coef = (1.2, 0.9, 1.5, 0.7, 1.1, 1.3, 0.8, 1.0)
ice_coef = (0.5, 1.4, 0.6, 1.2, 0.9, 0.4, 1.6, 0.7)
land_coef = (0.8, 1.1, 0.6, 1.5, 0.7, 1.2, 1.0, 0.5)

def bulk_flux(remapped, surface, factors):
    wind_speed = jnp.sqrt(1.0 + remapped[:, 0::3] * remapped[:, 0::3] + remapped[:, 1::3] * remapped[:, 1::3])
    weights = jnp.asarray(factors, jnp.float32)[None, :, None]
    return weights * wind_speed * (remapped[:, 2::3] - surface)

def to_blocks(array, count):
    return array.reshape(array.shape[0], count, BLOCK).transpose(1, 0, 2)

def remap_forward(atm_blocks, remote_map, local_map, tiles, device_count, per_device):
    offsets = (jnp.arange(device_count, dtype=jnp.int32) * AB_DEV)[:, None, None]
    remote_ids = remote_map.reshape(device_count, per_device, KR).astype(jnp.int32)
    local_ids = local_map.reshape(device_count, per_device, KL).astype(jnp.int32) + offsets
    targets = jnp.concatenate([remote_ids, local_ids], axis=2)
    tile_sets = tiles.reshape(device_count, per_device, KR + KL, BLOCK, BLOCK)

    def forward(operand):
        indices, tile_set = operand
        sources = atm_blocks[indices].astype(jnp.float32)
        return jnp.einsum('bkfs,bksd->bfd', sources, tile_set.astype(jnp.float32))
    mixed = lax.map(forward, (targets, tile_sets))
    return (targets, mixed.reshape(device_count * per_device, FIELDS, BLOCK))

def remap_back(flux, tiles, device_count, per_device):
    rounded = flux.astype(jnp.bfloat16).reshape(device_count, per_device, FLUXES, BLOCK)
    tile_sets = tiles.reshape(device_count, per_device, KR + KL, BLOCK, BLOCK)

    def backward(operand):
        flux_set, tile_set = operand
        return jnp.einsum('bfd,bksd->bkfs', flux_set.astype(jnp.float32), tile_set.astype(jnp.float32))
    terms = lax.map(backward, (rounded, tile_sets))
    return terms.reshape(-1, FLUXES * BLOCK)

def reference(atm_fields, ocn_state, ice_state, ice_level, lnd_state, lnd_level, ocn_map, ocn_local, ocn_tiles, lnd_map, lnd_local, lnd_tiles):
    device_count = N_SECT * N_CELL
    atm_blocks = to_blocks(atm_fields, NAB)
    ocean_targets, ocean_mixed = remap_forward(atm_blocks, ocn_map, ocn_local, ocn_tiles, device_count, OB_DEV)
    land_targets, land_mixed = remap_forward(atm_blocks, lnd_map, lnd_local, lnd_tiles, device_count, LB_DEV)
    ice_frac = (ice_level.astype(jnp.float32) / 8.0).reshape(NOB, 1, BLOCK)
    ocean_flux = (1.0 - ice_frac) * bulk_flux(ocean_mixed, to_blocks(ocn_state, NOB), ocean_coef) + ice_frac * bulk_flux(ocean_mixed, to_blocks(ice_state, NOB), ice_coef)
    land_frac = (lnd_level.astype(jnp.float32) / 8.0).reshape(NLB, 1, BLOCK)
    land_flux = land_frac * bulk_flux(land_mixed, to_blocks(lnd_state, NLB), land_coef)
    ocean_terms = remap_back(ocean_flux, ocn_tiles, device_count, OB_DEV)
    land_terms = remap_back(land_flux, lnd_tiles, device_count, LB_DEV)
    summed = jax.ops.segment_sum(ocean_terms, ocean_targets.reshape(-1), num_segments=NAB)
    summed = summed + jax.ops.segment_sum(land_terms, land_targets.reshape(-1), num_segments=NAB)
    atm_flux = summed.reshape(NAB, FLUXES, BLOCK).transpose(1, 0, 2).reshape(FLUXES, NA)
    ocn_flux = ocean_flux.transpose(1, 0, 2).reshape(FLUXES, NO)
    lnd_flux = land_flux.transpose(1, 0, 2).reshape(FLUXES, NL)
    return (atm_flux, ocn_flux, lnd_flux)
```

```python
import functools

import jax
import jax.numpy as jnp
from jax import lax
from jax.experimental import pallas as pl
from jax.experimental.pallas import tpu as pltpu
from jax.sharding import PartitionSpec as P

ocean_coef = (1.2, 0.9, 1.5, 0.7, 1.1, 1.3, 0.8, 1.0)
ice_coef = (0.5, 1.4, 0.6, 1.2, 0.9, 0.4, 1.6, 0.7)
land_coef = (0.8, 1.1, 0.6, 1.5, 0.7, 1.2, 1.0, 0.5)

BL = 128
AB = 32
CAP = 15
VMEM = pltpu.VMEM
SMEM = pltpu.SMEM
NN = (((1,), (0,)), ((), ()))
NT = (((1,), (1,)), ((), ()))


def dot(a, b, dims):
    return lax.dot_general(a, b, dims, preferred_element_type=jnp.float32)


def lanes(i):
    return pl.ds(pl.multiple_of(i * BL, BL), BL)


def whole(space=VMEM):
    return pl.BlockSpec(memory_space=space)


def column(values):
    row = lax.broadcasted_iota(jnp.int32, (8, BL), 0)
    out = jnp.full((8, BL), values[7], jnp.float32)
    for j in range(7):
        out = jnp.where(row == j, values[j], out)
    return out


def request_kernel(cells, om_ref, lm_ref, req_ref, slot_ref):
    sect = lax.axis_index("sect")
    before = jnp.zeros((cells, 1), jnp.float32)
    req = jnp.zeros((cells, BL), jnp.float32)
    slot_ref[...] = jnp.zeros(slot_ref.shape, jnp.int32)
    row = 0
    for ref in (om_ref, lm_ref):
        n = ref.shape[1]
        earlier = lax.broadcasted_iota(jnp.int32, (n, n), 0) < lax.broadcasted_iota(
            jnp.int32, (n, n), 1
        )
        earlier = jnp.where(earlier, 1.0, 0.0).astype(jnp.bfloat16)
        for k in range(ref.shape[0]):
            src = ref[k : k + 1, :]
            owner = src // AB
            col = owner % cells
            value = src % AB + jnp.where(owner // cells == sect, 0, AB)
            chosen = lax.broadcasted_iota(jnp.int32, (cells, n), 0) == col
            onehot = jnp.where(chosen, 1.0, 0.0)
            ranks = before + dot(onehot.astype(jnp.bfloat16), earlier, NN)
            rank = jnp.sum(jnp.where(chosen, ranks, 0.0), axis=0, keepdims=True)
            before = before + jnp.sum(onehot, axis=1, keepdims=True)
            place = lax.broadcasted_iota(jnp.int32, (BL, n), 0) == rank.astype(jnp.int32)
            place = jnp.where(place, 1.0, 0.0).astype(jnp.bfloat16)
            asked = jnp.where(chosen, (value + 1).astype(jnp.float32), 0.0)
            req = req + dot(asked.astype(jnp.bfloat16), place, NT)
            slot_ref[row : row + 1, :n] = col * CAP + rank.astype(jnp.int32)
            row += 1
    req_ref[...] = req.astype(jnp.int32) - 1


def requests(om, lm, cells):
    return pl.pallas_call(
        functools.partial(request_kernel, cells),
        out_shape=(
            jax.ShapeDtypeStruct((cells, BL), jnp.int32),
            jax.ShapeDtypeStruct((8, BL), jnp.int32),
        ),
        in_specs=[whole()] * 2,
        out_specs=[whole()] * 2,
        name="requests",
    )(om, lm)


def serve_kernel(cells, asked_ref, own_ref, near_ref, out_ref, both):
    width = own_ref.shape[1]
    both[:, :width] = own_ref[...]
    both[:, width:] = near_ref[...]

    def body(c, _):
        for r in range(CAP):
            i = jnp.maximum(asked_ref[c, r], 0)
            out_ref[c * CAP + r] = both[:, lanes(i)]
        return 0

    lax.fori_loop(0, cells, body, 0)


def serve(asked, own, near, cells):
    fields, width = own.shape
    return pl.pallas_call(
        functools.partial(serve_kernel, cells),
        out_shape=jax.ShapeDtypeStruct((cells * CAP, fields, BL), own.dtype),
        in_specs=[whole(SMEM), whole(), whole()],
        out_specs=whole(),
        scratch_shapes=[VMEM((fields, 2 * width), own.dtype)],
        compiler_params=pltpu.CompilerParams(vmem_limit_bytes=24 << 20),
        name="serve",
    )(asked, own, near)


STEPS = 8


def tile_specs(ob, lb, half):
    return [
        pl.BlockSpec((ob // STEPS, 2, BL, BL), lambda i: (i, half, 0, 0)),
        pl.BlockSpec((lb // STEPS, 2, BL, BL), lambda i: (i, half, 0, 0)),
    ]


def near_mix_kernel(ol_ref, ll_ref, f_ref, ot_ref, lt_ref, om_ref, lm_ref):
    step = pl.program_id(0)
    for ids, tiles, out in ((ol_ref, ot_ref, om_ref), (ll_ref, lt_ref, lm_ref)):
        n = tiles.shape[0]
        for b in range(n):
            src = [f_ref[:, lanes(ids[k, step * n + b])] for k in range(2)]
            out[b] = dot(
                jnp.concatenate(src, axis=1), tiles[b].reshape(2 * BL, BL), NN
            )


def near_mix(ol, ll, fields, ot, lt):
    ob, lb = ot.shape[0], lt.shape[0]
    nf = fields.shape[0]
    return pl.pallas_call(
        near_mix_kernel,
        grid=(STEPS,),
        out_shape=(
            jax.ShapeDtypeStruct((ob, nf, BL), jnp.float32),
            jax.ShapeDtypeStruct((lb, nf, BL), jnp.float32),
        ),
        in_specs=[
            whole(SMEM),
            whole(SMEM),
            pl.BlockSpec(fields.shape, lambda i: (0, 0)),
            *tile_specs(ob, lb, 1),
        ],
        out_specs=[
            pl.BlockSpec((ob // STEPS, nf, BL), lambda i: (i, 0, 0)),
            pl.BlockSpec((lb // STEPS, nf, BL), lambda i: (i, 0, 0)),
        ],
        compiler_params=pltpu.CompilerParams(vmem_limit_bytes=24 << 20),
        cost_estimate=pl.CostEstimate(
            flops=2 * (ob + lb) * 2 * BL * BL * 128,
            bytes_accessed=(ob + lb) * 2 * BL * BL * 2,
            transcendentals=0,
        ),
        name="near_mix",
    )(ol, ll, fields, ot, lt)


def far_kernel(
    slot_ref, got_ref, ot_ref, lt_ref, om_ref, lm_ref, os_ref, is_ref, il_ref, ls_ref, ll_ref,
    of_ref, lf_ref, send_ref, mixed,
):
    step = pl.program_id(0)

    @pl.when(step == 0)
    def _():
        send_ref[...] = jnp.zeros(send_ref.shape, send_ref.dtype)

    ocean, ice, land = column(ocean_coef), column(ice_coef), column(land_coef)
    no, nl = ot_ref.shape[0], lt_ref.shape[0]
    for b in range(no + nl):
        is_ocean = b < no
        tiles, near = (ot_ref, om_ref) if is_ocean else (lt_ref, lm_ref)
        c = b if is_ocean else b - no
        base = 0 if is_ocean else 2
        at = step * (no if is_ocean else nl) + c
        slots = [slot_ref[base + k, at] for k in range(2)]
        weights = tiles[c].reshape(2 * BL, BL)
        src = jnp.concatenate([got_ref[s] for s in slots], axis=1)
        mixed[b] = near[c] + dot(src, weights, NN)
        u = mixed[b, pl.ds(0, 8, stride=3), :]
        v = mixed[b, pl.ds(1, 8, stride=3), :]
        t = mixed[b, pl.ds(2, 8, stride=3), :]
        wind = jnp.sqrt(1.0 + u * u + v * v)
        here = slice(c * BL, (c + 1) * BL)
        if is_ocean:
            frac = il_ref[c : c + 1, :].astype(jnp.float32) / 8.0
            flux = (1.0 - frac) * (ocean * wind * (t - os_ref[:, here]))
            flux = flux + frac * (ice * wind * (t - is_ref[:, here]))
            of_ref[:, here] = flux
        else:
            frac = ll_ref[pl.ds(at, 1), :].astype(jnp.float32) / 8.0
            flux = frac * (land * wind * (t - ls_ref[:, here]))
            lf_ref[:, here] = flux
        terms = dot(flux.astype(jnp.bfloat16), weights, NT).astype(send_ref.dtype)
        for k in range(2):
            send_ref[slots[k]] = terms[:, k * BL : (k + 1) * BL]


def far(slots, got, ot, lt, om, lm, os, ice, il, ls, ll):
    ob, lb = ot.shape[0], lt.shape[0]
    nf, ns = om.shape[1], os.shape[0]
    no, nl = ob // STEPS, lb // STEPS
    return pl.pallas_call(
        far_kernel,
        grid=(STEPS,),
        out_shape=(
            jax.ShapeDtypeStruct(os.shape, jnp.float32),
            jax.ShapeDtypeStruct(ls.shape, jnp.float32),
            jax.ShapeDtypeStruct((got.shape[0], ns, BL), jnp.bfloat16),
        ),
        in_specs=[
            whole(SMEM),
            pl.BlockSpec(got.shape, lambda i: (0, 0, 0)),
            *tile_specs(ob, lb, 0),
            pl.BlockSpec((no, nf, BL), lambda i: (i, 0, 0)),
            pl.BlockSpec((nl, nf, BL), lambda i: (i, 0, 0)),
            pl.BlockSpec((ns, no * BL), lambda i: (0, i)),
            pl.BlockSpec((ns, no * BL), lambda i: (0, i)),
            pl.BlockSpec((no, BL), lambda i: (i, 0)),
            pl.BlockSpec((ns, nl * BL), lambda i: (0, i)),
            pl.BlockSpec((lb, BL), lambda i: (0, 0)),
        ],
        out_specs=[
            pl.BlockSpec((ns, no * BL), lambda i: (0, i)),
            pl.BlockSpec((ns, nl * BL), lambda i: (0, i)),
            pl.BlockSpec((got.shape[0], ns, BL), lambda i: (0, 0, 0)),
        ],
        scratch_shapes=[VMEM((no + nl, nf, BL), jnp.float32)],
        compiler_params=pltpu.CompilerParams(vmem_limit_bytes=32 << 20),
        name="far",
    )(slots, got, ot, lt, om, lm, os, ice, il, ls, ll)


def near_back_kernel(ol_ref, ll_ref, of_ref, lf_ref, ot_ref, lt_ref, out_ref):
    step = pl.program_id(0)

    @pl.when(step == 0)
    def _():
        out_ref[...] = jnp.zeros(out_ref.shape, out_ref.dtype)

    for ids, flux, tiles in ((ol_ref, of_ref, ot_ref), (ll_ref, lf_ref, lt_ref)):
        n = tiles.shape[0]
        for b in range(n):
            g = flux[:, b * BL : (b + 1) * BL].astype(jnp.bfloat16)
            terms = dot(g, tiles[b].reshape(2 * BL, BL), NT)
            for k in range(2):
                at = lanes(ids[k, step * n + b])
                out_ref[:, at] = out_ref[:, at] + terms[:, k * BL : (k + 1) * BL]


def near_back(ol, ll, of, lf, ot, lt):
    ob, lb = ot.shape[0], lt.shape[0]
    ns = of.shape[0]
    return pl.pallas_call(
        near_back_kernel,
        grid=(STEPS,),
        out_shape=jax.ShapeDtypeStruct((ns, AB * BL), jnp.float32),
        in_specs=[
            whole(SMEM),
            whole(SMEM),
            pl.BlockSpec((ns, ob // STEPS * BL), lambda i: (0, i)),
            pl.BlockSpec((ns, lb // STEPS * BL), lambda i: (0, i)),
            *tile_specs(ob, lb, 1),
        ],
        out_specs=pl.BlockSpec((ns, AB * BL), lambda i: (0, 0)),
        compiler_params=pltpu.CompilerParams(vmem_limit_bytes=24 << 20),
        cost_estimate=pl.CostEstimate(
            flops=2 * (ob + lb) * 2 * BL * BL * 128,
            bytes_accessed=(ob + lb) * 2 * BL * BL * 2,
            transcendentals=0,
        ),
        name="near_back",
    )(ol, ll, of, lf, ot, lt)


def collect_kernel(cells, neighbours, asked_ref, back_ref, *refs):
    acc_refs, out_ref, total = refs[:-2], refs[-2], refs[-1]
    cell = lax.axis_index("cell")
    half = cells // 2
    width = out_ref.shape[1]
    if acc_refs:
        total[:, :width] = acc_refs[0][...]
    else:
        total[:, :width] = jnp.zeros((total.shape[0], width), jnp.float32)

    def body(c, _):
        far_one = jnp.logical_or(c <= cell - half, c > cell + half)

        @pl.when(far_one == neighbours)
        def _():
            for r in range(CAP):
                i = asked_ref[c, r]
                at = lanes(jnp.where(i < 0, AB, lax.rem(i, AB)))
                total[:, at] = total[:, at] + back_ref[c * CAP + r].astype(jnp.float32)

        return 0

    lax.fori_loop(0, cells, body, 0)
    out_ref[...] = total[:, :width]


def collect(asked, back, acc, neighbours, cells):
    ns = back.shape[1]
    accs = () if acc is None else (acc,)
    return pl.pallas_call(
        functools.partial(collect_kernel, cells, neighbours),
        out_shape=jax.ShapeDtypeStruct((ns, AB * BL), jnp.float32),
        in_specs=[whole(SMEM), whole(), *[whole()] * len(accs)],
        out_specs=whole(),
        scratch_shapes=[VMEM((ns, (AB + 1) * BL), jnp.float32)],
        cost_estimate=pl.CostEstimate(
            flops=1 << 20, bytes_accessed=4 << 20, transcendentals=0
        ),
        name="collect_far" if neighbours else "collect_own",
    )(asked, back, *accs)


def per_device(
    sects, cells, atm_fields, ocn_state, ice_state, ice_level, lnd_state, lnd_level,
    ocn_map, ocn_local, ocn_tiles, lnd_map, lnd_local, lnd_tiles,
):
    axes = ("sect", "cell")
    count = sects * cells
    half = cells // 2
    to_server = []
    for q in range(count):
        s, c = divmod(q, cells)
        to_server.append((q, (s + (1 if c >= half else -1)) % sects * cells + c))
    to_owner = [(b, a) for a, b in to_server]
    exchange = functools.partial(
        lax.all_to_all, axis_name="cell", split_axis=0, concat_axis=0, tiled=True
    )

    near_fields = lax.ppermute(atm_fields, axes, to_server)
    asking, slots = requests(ocn_map.T, lnd_map.T, cells)
    asked = exchange(asking)
    got = exchange(serve(asked, atm_fields, near_fields, cells))
    ol, ll = ocn_local.T, lnd_local.T
    om, lm = near_mix(ol, ll, atm_fields, ocn_tiles, lnd_tiles)
    of, lf, send = far(
        slots, got, ocn_tiles, lnd_tiles, om, lm, ocn_state, ice_state,
        ice_level.reshape(-1, BL), lnd_state, lnd_level.reshape(-1, BL),
    )
    back = exchange(send)
    acc = near_back(ol, ll, of, lf, ocn_tiles, lnd_tiles)
    away = lax.ppermute(collect(asked, back, None, True, cells), axes, to_owner)
    own = collect(asked, back, acc, False, cells)
    return own + away, of, lf


def solution(mesh):
    a = ("sect", "cell")
    in_specs = (
        P(None, a), P(None, a), P(None, a), P(a), P(None, a), P(a),
        P(a, None), P(a, None), P(a, None, None, None),
        P(a, None), P(a, None), P(a, None, None, None),
    )
    return jax.shard_map(
        functools.partial(per_device, mesh.shape["sect"], mesh.shape["cell"]),
        mesh=mesh,
        in_specs=in_specs,
        out_specs=(P(None, a), P(None, a), P(None, a)),
        check_vma=False,
    )
```

```python
import functools

import jax
import jax.numpy as jnp
from jax import lax
from jax.experimental import pallas as pl
from jax.experimental.pallas import tpu as pltpu
from jax.sharding import PartitionSpec as P

ocean_coef = (1.2, 0.9, 1.5, 0.7, 1.1, 1.3, 0.8, 1.0)
ice_coef = (0.5, 1.4, 0.6, 1.2, 0.9, 0.4, 1.6, 0.7)
land_coef = (0.8, 1.1, 0.6, 1.5, 0.7, 1.2, 1.0, 0.5)

BL = 128
AB = 32
CAP = 15
GRANT = 60 << 20
CHAINS = 5
VMEM = pltpu.VMEM
SMEM = pltpu.SMEM
NN = (((1,), (0,)), ((), ()))
NT = (((1,), (1,)), ((), ()))


def dot(a, b, dims):
    return lax.dot_general(a, b, dims, preferred_element_type=jnp.float32)


def lanes(i):
    return pl.ds(pl.multiple_of(i * BL, BL), BL)


def whole(space=VMEM):
    return pl.BlockSpec(memory_space=space)


def column(values):
    row = lax.broadcasted_iota(jnp.int32, (8, BL), 0)
    out = jnp.full((8, BL), values[7], jnp.float32)
    for j in range(7):
        out = jnp.where(row == j, values[j], out)
    return out


def request_kernel(cells, om_ref, lm_ref, req_ref, slot_ref):
    sect = lax.axis_index("sect")
    before = jnp.zeros((cells, 1), jnp.float32)
    req = jnp.zeros((cells, BL), jnp.float32)
    slot_ref[...] = jnp.zeros(slot_ref.shape, jnp.int32)
    row = 0
    for ref in (om_ref, lm_ref):
        n = ref.shape[1]
        earlier = lax.broadcasted_iota(jnp.int32, (n, n), 0) < lax.broadcasted_iota(
            jnp.int32, (n, n), 1
        )
        earlier = jnp.where(earlier, 1.0, 0.0).astype(jnp.bfloat16)
        for k in range(ref.shape[0]):
            src = ref[k : k + 1, :]
            owner = src // AB
            col = owner % cells
            value = src % AB + jnp.where(owner // cells == sect, 0, AB)
            chosen = lax.broadcasted_iota(jnp.int32, (cells, n), 0) == col
            onehot = jnp.where(chosen, 1.0, 0.0)
            ranks = before + dot(onehot.astype(jnp.bfloat16), earlier, NN)
            rank = jnp.sum(jnp.where(chosen, ranks, 0.0), axis=0, keepdims=True)
            before = before + jnp.sum(onehot, axis=1, keepdims=True)
            place = lax.broadcasted_iota(jnp.int32, (BL, n), 0) == rank.astype(jnp.int32)
            place = jnp.where(place, 1.0, 0.0).astype(jnp.bfloat16)
            asked = jnp.where(chosen, (value + 1).astype(jnp.float32), 0.0)
            req = req + dot(asked.astype(jnp.bfloat16), place, NT)
            slot_ref[row : row + 1, :n] = col * CAP + rank.astype(jnp.int32)
            row += 1
    req_ref[...] = req.astype(jnp.int32) - 1


def requests(om, lm, cells):
    return pl.pallas_call(
        functools.partial(request_kernel, cells),
        out_shape=(
            jax.ShapeDtypeStruct((cells, BL), jnp.int32),
            jax.ShapeDtypeStruct((8, BL), jnp.int32),
        ),
        in_specs=[whole()] * 2,
        out_specs=[whole()] * 2,
        compiler_params=pltpu.CompilerParams(vmem_limit_bytes=GRANT),
        name="requests",
    )(om, lm)


def serve_kernel(cells, asked_ref, own_ref, near_ref, out_ref, both):
    width = own_ref.shape[1]
    both[:, :width] = own_ref[...]
    both[:, width:] = near_ref[...]

    def body(c, _):
        for r in range(CAP):
            i = jnp.maximum(asked_ref[c, r], 0)
            out_ref[c * CAP + r] = both[:, lanes(i)]
        return 0

    lax.fori_loop(0, cells, body, 0)


def serve(asked, own, near, cells):
    fields, width = own.shape
    return pl.pallas_call(
        functools.partial(serve_kernel, cells),
        out_shape=jax.ShapeDtypeStruct((cells * CAP, fields, BL), own.dtype),
        in_specs=[whole(SMEM), whole(), whole()],
        out_specs=whole(),
        scratch_shapes=[VMEM((fields, 2 * width), own.dtype)],
        compiler_params=pltpu.CompilerParams(vmem_limit_bytes=GRANT),
        name="serve",
    )(asked, own, near)


STEPS = 4


def tile_specs(ob, lb, half):
    return [
        pl.BlockSpec((ob // STEPS, 2, BL, BL), lambda i: (i, half, 0, 0)),
        pl.BlockSpec((lb // STEPS, 2, BL, BL), lambda i: (i, half, 0, 0)),
    ]


def near_mix_kernel(ol_ref, ll_ref, f_ref, ot_ref, lt_ref, om_ref, lm_ref):
    step = pl.program_id(0)
    for ids, tiles, out in ((ol_ref, ot_ref, om_ref), (ll_ref, lt_ref, lm_ref)):
        n = tiles.shape[0]
        for b in range(n):
            src = [f_ref[:, lanes(ids[k, step * n + b])] for k in range(2)]
            out[b] = dot(
                jnp.concatenate(src, axis=1), tiles[b].reshape(2 * BL, BL), NN
            )


def near_mix(ol, ll, fields, ot, lt):
    ob, lb = ot.shape[0], lt.shape[0]
    nf = fields.shape[0]
    return pl.pallas_call(
        near_mix_kernel,
        grid=(STEPS,),
        out_shape=(
            jax.ShapeDtypeStruct((ob, nf, BL), jnp.float32),
            jax.ShapeDtypeStruct((lb, nf, BL), jnp.float32),
        ),
        in_specs=[
            whole(SMEM),
            whole(SMEM),
            pl.BlockSpec(fields.shape, lambda i: (0, 0)),
            *tile_specs(ob, lb, 1),
        ],
        out_specs=[
            pl.BlockSpec((ob // STEPS, nf, BL), lambda i: (i, 0, 0)),
            pl.BlockSpec((lb // STEPS, nf, BL), lambda i: (i, 0, 0)),
        ],
        compiler_params=pltpu.CompilerParams(vmem_limit_bytes=GRANT),
        cost_estimate=pl.CostEstimate(
            flops=2 * (ob + lb) * 2 * BL * BL * 128,
            bytes_accessed=(ob + lb) * 2 * BL * BL * 2,
            transcendentals=0,
        ),
        name="near_mix",
    )(ol, ll, fields, ot, lt)


def far_kernel(
    slot_ref, got_ref, ot_ref, lt_ref, om_ref, lm_ref, os_ref, is_ref, il_ref, ls_ref, ll_ref,
    of_ref, lf_ref, send_ref, mixed,
):
    step = pl.program_id(0)

    @pl.when(step == 0)
    def _():
        send_ref[...] = jnp.zeros(send_ref.shape, send_ref.dtype)

    ocean, ice, land = column(ocean_coef), column(ice_coef), column(land_coef)
    no, nl = ot_ref.shape[0], lt_ref.shape[0]
    blocks = []
    for b in range(no + nl):
        is_ocean = b < no
        c = b if is_ocean else b - no
        at = step * (no if is_ocean else nl) + c
        slots = [slot_ref[(0 if is_ocean else 2) + k, at] for k in range(2)]
        blocks.append((is_ocean, c, at, slots))
    for b, (is_ocean, c, at, slots) in enumerate(blocks):
        tiles, near = (ot_ref, om_ref) if is_ocean else (lt_ref, lm_ref)
        src = jnp.concatenate([got_ref[s] for s in slots], axis=1)
        mixed[b] = near[c] + dot(src, tiles[c].reshape(2 * BL, BL), NN)
    for b, (is_ocean, c, at, slots) in enumerate(blocks):
        u = mixed[b, pl.ds(0, 8, stride=3), :]
        v = mixed[b, pl.ds(1, 8, stride=3), :]
        t = mixed[b, pl.ds(2, 8, stride=3), :]
        wind = jnp.sqrt(1.0 + u * u + v * v)
        here = slice(c * BL, (c + 1) * BL)
        if is_ocean:
            frac = il_ref[c : c + 1, :].astype(jnp.float32) / 8.0
            flux = (1.0 - frac) * (ocean * wind * (t - os_ref[:, here]))
            flux = flux + frac * (ice * wind * (t - is_ref[:, here]))
            of_ref[:, here] = flux
        else:
            frac = ll_ref[pl.ds(at, 1), :].astype(jnp.float32) / 8.0
            flux = frac * (land * wind * (t - ls_ref[:, here]))
            lf_ref[:, here] = flux
    for b, (is_ocean, c, at, slots) in enumerate(blocks):
        tiles, flux = (ot_ref, of_ref) if is_ocean else (lt_ref, lf_ref)
        here = slice(c * BL, (c + 1) * BL)
        terms = dot(flux[:, here].astype(jnp.bfloat16), tiles[c].reshape(2 * BL, BL), NT)
        terms = terms.astype(send_ref.dtype)
        for k in range(2):
            send_ref[slots[k]] = terms[:, k * BL : (k + 1) * BL]


def far(slots, got, ot, lt, om, lm, os, ice, il, ls, ll):
    ob, lb = ot.shape[0], lt.shape[0]
    nf, ns = om.shape[1], os.shape[0]
    no, nl = ob // STEPS, lb // STEPS
    return pl.pallas_call(
        far_kernel,
        grid=(STEPS,),
        out_shape=(
            jax.ShapeDtypeStruct(os.shape, jnp.float32),
            jax.ShapeDtypeStruct(ls.shape, jnp.float32),
            jax.ShapeDtypeStruct((got.shape[0], ns, BL), jnp.bfloat16),
        ),
        in_specs=[
            whole(SMEM),
            pl.BlockSpec(got.shape, lambda i: (0, 0, 0)),
            *tile_specs(ob, lb, 0),
            pl.BlockSpec((no, nf, BL), lambda i: (i, 0, 0)),
            pl.BlockSpec((nl, nf, BL), lambda i: (i, 0, 0)),
            pl.BlockSpec((ns, no * BL), lambda i: (0, i)),
            pl.BlockSpec((ns, no * BL), lambda i: (0, i)),
            pl.BlockSpec((no, BL), lambda i: (i, 0)),
            pl.BlockSpec((ns, nl * BL), lambda i: (0, i)),
            pl.BlockSpec((lb, BL), lambda i: (0, 0)),
        ],
        out_specs=[
            pl.BlockSpec((ns, no * BL), lambda i: (0, i)),
            pl.BlockSpec((ns, nl * BL), lambda i: (0, i)),
            pl.BlockSpec((got.shape[0], ns, BL), lambda i: (0, 0, 0)),
        ],
        scratch_shapes=[VMEM((no + nl, nf, BL), jnp.float32)],
        compiler_params=pltpu.CompilerParams(vmem_limit_bytes=GRANT),
        name="far",
    )(slots, got, ot, lt, om, lm, os, ice, il, ls, ll)


def near_back_kernel(ol_ref, ll_ref, of_ref, lf_ref, ot_ref, lt_ref, out_ref):
    step = pl.program_id(0)

    @pl.when(step == 0)
    def _():
        out_ref[...] = jnp.zeros(out_ref.shape, out_ref.dtype)

    for ids, flux, tiles in ((ol_ref, of_ref, ot_ref), (ll_ref, lf_ref, lt_ref)):
        n = tiles.shape[0]
        for b in range(n):
            g = flux[:, b * BL : (b + 1) * BL].astype(jnp.bfloat16)
            terms = dot(g, tiles[b].reshape(2 * BL, BL), NT)
            for k in range(2):
                at = lanes(ids[k, step * n + b])
                out_ref[:, at] = out_ref[:, at] + terms[:, k * BL : (k + 1) * BL]


def near_back(ol, ll, of, lf, ot, lt):
    ob, lb = ot.shape[0], lt.shape[0]
    ns = of.shape[0]
    return pl.pallas_call(
        near_back_kernel,
        grid=(STEPS,),
        out_shape=jax.ShapeDtypeStruct((ns, AB * BL), jnp.float32),
        in_specs=[
            whole(SMEM),
            whole(SMEM),
            pl.BlockSpec((ns, ob // STEPS * BL), lambda i: (0, i)),
            pl.BlockSpec((ns, lb // STEPS * BL), lambda i: (0, i)),
            *tile_specs(ob, lb, 1),
        ],
        out_specs=pl.BlockSpec((ns, AB * BL), lambda i: (0, 0)),
        compiler_params=pltpu.CompilerParams(vmem_limit_bytes=GRANT),
        cost_estimate=pl.CostEstimate(
            flops=2 * (ob + lb) * 2 * BL * BL * 128,
            bytes_accessed=(ob + lb) * 2 * BL * BL * 2,
            transcendentals=0,
        ),
        name="near_back",
    )(ol, ll, of, lf, ot, lt)


def collect_kernel(cells, neighbours, asked_ref, back_ref, *refs):
    acc_refs, out_ref, totals = refs[: -1 - CHAINS], refs[-1 - CHAINS], refs[-CHAINS:]
    cell = lax.axis_index("cell")
    half = cells // 2
    for total in totals:
        total[...] = jnp.zeros(total.shape, jnp.float32)

    def body(c, _):
        far_one = jnp.logical_or(c <= cell - half, c > cell + half)

        @pl.when(far_one == neighbours)
        def _():
            for r in range(CAP):
                total = totals[r % CHAINS]
                i = asked_ref[c, r]
                at = lanes(jnp.where(i < 0, AB, i & (AB - 1)))
                total[:, at] = total[:, at] + back_ref[c * CAP + r].astype(jnp.float32)

        return 0

    lax.fori_loop(0, cells, body, 0)
    for b in range(AB):
        here = slice(b * BL, (b + 1) * BL)
        parts = [ref[:, here] for ref in (*acc_refs, *totals)]
        out_ref[:, here] = functools.reduce(jnp.add, parts)


def collect(asked, back, acc, neighbours, cells):
    ns = back.shape[1]
    accs = () if acc is None else (acc,)
    return pl.pallas_call(
        functools.partial(collect_kernel, cells, neighbours),
        out_shape=jax.ShapeDtypeStruct((ns, AB * BL), jnp.float32),
        in_specs=[whole(SMEM), whole(), *[whole()] * len(accs)],
        out_specs=whole(),
        scratch_shapes=[VMEM((ns, (AB + 1) * BL), jnp.float32)] * CHAINS,
        compiler_params=pltpu.CompilerParams(vmem_limit_bytes=GRANT),
        cost_estimate=pl.CostEstimate(
            flops=1 << 20, bytes_accessed=4 << 20, transcendentals=0
        ),
        name="collect_far" if neighbours else "collect_own",
    )(asked, back, *accs)


def per_device(
    sects, cells, atm_fields, ocn_state, ice_state, ice_level, lnd_state, lnd_level,
    ocn_map, ocn_local, ocn_tiles, lnd_map, lnd_local, lnd_tiles,
):
    axes = ("sect", "cell")
    count = sects * cells
    half = cells // 2
    to_server = []
    for q in range(count):
        s, c = divmod(q, cells)
        to_server.append((q, (s + (1 if c >= half else -1)) % sects * cells + c))
    to_owner = [(b, a) for a, b in to_server]
    exchange = functools.partial(
        lax.all_to_all, axis_name="cell", split_axis=0, concat_axis=0, tiled=True
    )

    near_fields = lax.ppermute(atm_fields, axes, to_server)
    asking, slots = requests(ocn_map.T, lnd_map.T, cells)
    asked = exchange(asking)
    got = exchange(serve(asked, atm_fields, near_fields, cells))
    ol, ll = ocn_local.T, lnd_local.T
    om, lm = near_mix(ol, ll, atm_fields, ocn_tiles, lnd_tiles)
    of, lf, send = far(
        slots, got, ocn_tiles, lnd_tiles, om, lm, ocn_state, ice_state,
        ice_level.reshape(-1, BL), lnd_state, lnd_level.reshape(-1, BL),
    )
    back = exchange(send)
    acc = near_back(ol, ll, of, lf, ocn_tiles, lnd_tiles)
    back, acc = lax.optimization_barrier((back, acc))
    away = lax.ppermute(collect(asked, back, None, True, cells), axes, to_owner)
    own = collect(asked, back, acc, False, cells)
    return own + away, of, lf


def solution(mesh):
    a = ("sect", "cell")
    in_specs = (
        P(None, a), P(None, a), P(None, a), P(a), P(None, a), P(a),
        P(a, None), P(a, None), P(a, None, None, None),
        P(a, None), P(a, None), P(a, None, None, None),
    )
    return jax.shard_map(
        functools.partial(per_device, mesh.shape["sect"], mesh.shape["cell"]),
        mesh=mesh,
        in_specs=in_specs,
        out_specs=(P(None, a), P(None, a), P(None, a)),
        check_vma=False,
    )
```

```python
import functools

import jax
import jax.numpy as jnp
from jax import lax
from jax.experimental import pallas as pl
from jax.experimental.pallas import tpu as pltpu
from jax.sharding import PartitionSpec as P

ocean_coef = (1.2, 0.9, 1.5, 0.7, 1.1, 1.3, 0.8, 1.0)
ice_coef = (0.5, 1.4, 0.6, 1.2, 0.9, 0.4, 1.6, 0.7)
land_coef = (0.8, 1.1, 0.6, 1.5, 0.7, 1.2, 1.0, 0.5)

BL = 128
AB = 32
CAP = 15
GRANT, LARGE, SMALL = 60 << 20, 50 << 20, 8 << 20
CHAINS = 5
VMEM = pltpu.VMEM
SMEM = pltpu.SMEM
NN = (((1,), (0,)), ((), ()))
NT = (((1,), (1,)), ((), ()))


def dot(a, b, dims):
    return lax.dot_general(a, b, dims, preferred_element_type=jnp.float32)


def lanes(i):
    return pl.ds(pl.multiple_of(i * BL, BL), BL)


def whole(space=VMEM):
    return pl.BlockSpec(memory_space=space)


def column(values):
    row = lax.broadcasted_iota(jnp.int32, (8, BL), 0)
    out = jnp.full((8, BL), values[7], jnp.float32)
    for j in range(7):
        out = jnp.where(row == j, values[j], out)
    return out


def request_kernel(cells, om_ref, lm_ref, req_ref, slot_ref):
    sect = lax.axis_index("sect")
    before = jnp.zeros((cells, 1), jnp.float32)
    req = jnp.zeros((cells, BL), jnp.float32)
    slot_ref[...] = jnp.zeros(slot_ref.shape, jnp.int32)
    row = 0
    for ref in (om_ref, lm_ref):
        n = ref.shape[1]
        earlier = lax.broadcasted_iota(jnp.int32, (n, n), 0) < lax.broadcasted_iota(
            jnp.int32, (n, n), 1
        )
        earlier = jnp.where(earlier, 1.0, 0.0).astype(jnp.bfloat16)
        for k in range(ref.shape[0]):
            src = ref[k : k + 1, :]
            owner = src // AB
            col = owner % cells
            value = src % AB + jnp.where(owner // cells == sect, 0, AB)
            chosen = lax.broadcasted_iota(jnp.int32, (cells, n), 0) == col
            onehot = jnp.where(chosen, 1.0, 0.0)
            ranks = before + dot(onehot.astype(jnp.bfloat16), earlier, NN)
            rank = jnp.sum(jnp.where(chosen, ranks, 0.0), axis=0, keepdims=True)
            before = before + jnp.sum(onehot, axis=1, keepdims=True)
            place = lax.broadcasted_iota(jnp.int32, (BL, n), 0) == rank.astype(jnp.int32)
            place = jnp.where(place, 1.0, 0.0).astype(jnp.bfloat16)
            asked = jnp.where(chosen, (value + 1).astype(jnp.float32), 0.0)
            req = req + dot(asked.astype(jnp.bfloat16), place, NT)
            slot_ref[row : row + 1, :n] = col * CAP + rank.astype(jnp.int32)
            row += 1
    req_ref[...] = req.astype(jnp.int32) - 1


def requests(om, lm, cells):
    return pl.pallas_call(
        functools.partial(request_kernel, cells),
        out_shape=(
            jax.ShapeDtypeStruct((cells, BL), jnp.int32),
            jax.ShapeDtypeStruct((8, BL), jnp.int32),
        ),
        in_specs=[whole()] * 2,
        out_specs=[whole()] * 2,
        compiler_params=pltpu.CompilerParams(vmem_limit_bytes=GRANT),
        name="requests",
    )(om, lm)


def hold_kernel(own_ref, near_ref, out_ref, sems):
    width = own_ref.shape[1]
    copies = [
        pltpu.make_async_copy(ref, out_ref.at[:, pl.ds(k * width, width)], sems.at[k])
        for k, ref in enumerate((own_ref, near_ref))
    ]
    for copy in copies:
        copy.start()
    for copy in copies:
        copy.wait()


def hold(own, near):
    return pl.pallas_call(
        hold_kernel,
        out_shape=jax.ShapeDtypeStruct((own.shape[0], 2 * own.shape[1]), own.dtype),
        in_specs=[whole(pl.ANY)] * 2,
        out_specs=whole(),
        scratch_shapes=[pltpu.SemaphoreType.DMA((2,))],
        compiler_params=pltpu.CompilerParams(vmem_limit_bytes=SMALL),
        cost_estimate=pl.CostEstimate(flops=1 << 20, bytes_accessed=4 << 20, transcendentals=0),
        name="hold",
    )(own, near)


def serve_kernel(cells, asked_ref, both, out_ref, made, out_sems):
    def out(c):
        part = pl.ds(c * CAP, CAP)
        return pltpu.make_async_copy(made.at[part], out_ref.at[part], out_sems.at[c])

    def body(c, _):
        for r in range(CAP):
            i = jnp.maximum(asked_ref[c, r], 0)
            made[c * CAP + r] = both[:, lanes(i)]
        out(c).start()
        return 0

    lax.fori_loop(0, cells, body, 0)
    for c in range(cells):
        out(c).wait()


def serve(asked, both, cells):
    shape = (cells * CAP, both.shape[0], BL)
    return pl.pallas_call(
        functools.partial(serve_kernel, cells),
        out_shape=jax.ShapeDtypeStruct(shape, both.dtype),
        in_specs=[whole(SMEM), whole()],
        out_specs=whole(pltpu.HBM),
        scratch_shapes=[VMEM(shape, both.dtype), pltpu.SemaphoreType.DMA((cells,))],
        compiler_params=pltpu.CompilerParams(vmem_limit_bytes=SMALL),
        name="serve",
    )(asked, both)


STEPS = 4


def tile_specs(ob, lb, half):
    return [
        pl.BlockSpec((ob // STEPS, 2, BL, BL), lambda i: (i, half, 0, 0)),
        pl.BlockSpec((lb // STEPS, 2, BL, BL), lambda i: (i, half, 0, 0)),
    ]


def near_mix_kernel(ol_ref, ll_ref, f_ref, ot_ref, lt_ref, out_ref):
    step = pl.program_id(0)
    at = 0
    for ids, tiles in ((ol_ref, ot_ref), (ll_ref, lt_ref)):
        n = tiles.shape[0]
        for b in range(n):
            src = [f_ref[:, lanes(ids[k, step * n + b])] for k in range(2)]
            out_ref[at] = dot(
                jnp.concatenate(src, axis=1), tiles[b].reshape(2 * BL, BL), NN
            )
            at += 1


def near_mix(ol, ll, fields, ot, lt):
    ob, lb = ot.shape[0], lt.shape[0]
    nf = fields.shape[0]
    return pl.pallas_call(
        near_mix_kernel,
        grid=(STEPS,),
        out_shape=jax.ShapeDtypeStruct((ob + lb, nf, BL), jnp.float32),
        in_specs=[
            whole(SMEM),
            whole(SMEM),
            pl.BlockSpec(fields.shape, lambda i: (0, 0)),
            *tile_specs(ob, lb, 1),
        ],
        out_specs=pl.BlockSpec(((ob + lb) // STEPS, nf, BL), lambda i: (i, 0, 0)),
        compiler_params=pltpu.CompilerParams(vmem_limit_bytes=GRANT),
        cost_estimate=pl.CostEstimate(
            flops=2 * (ob + lb) * 2 * BL * BL * 128,
            bytes_accessed=(ob + lb) * 2 * BL * BL * 2,
            transcendentals=0,
        ),
        name="near_mix",
    )(ol, ll, fields, ot, lt)


def far_kernel(
    slot_ref, got_hbm, ot_hbm, lt_hbm, near_hbm, os_hbm, is_hbm, il_hbm, ls_hbm, ll_hbm,
    of_hbm, lf_hbm, send_hbm,
    got_ref, ot, lt, near, osv, isv, il, ls, ll, of, lf, send, mixed, in_sems, out_sems,
):
    no, nl = ot.shape[0] // STEPS, lt.shape[0] // STEPS

    def ins(i):
        o, l, n = pl.ds(i * no, no), pl.ds(i * nl, nl), pl.ds(i * (no + nl), no + nl)
        ow = pl.ds(pl.multiple_of(i * no * BL, no * BL), no * BL)
        lw = pl.ds(pl.multiple_of(i * nl * BL, nl * BL), nl * BL)
        pairs = (
            (ot_hbm.at[o, pl.ds(0, 2)], ot.at[o]),
            (lt_hbm.at[l, pl.ds(0, 2)], lt.at[l]),
            (near_hbm.at[n], near.at[n]),
            (os_hbm.at[:, ow], osv.at[:, ow]),
            (is_hbm.at[:, ow], isv.at[:, ow]),
            (ls_hbm.at[:, lw], ls.at[:, lw]),
        )
        return [
            pltpu.make_async_copy(a, b, in_sems.at[k, i]) for k, (a, b) in enumerate(pairs)
        ]

    levels = [
        pltpu.make_async_copy(a, b, in_sems.at[6, k])
        for k, (a, b) in enumerate(((got_hbm, got_ref), (il_hbm, il), (ll_hbm, ll)))
    ]
    for copy in levels:
        copy.start()
    for i in range(STEPS):
        for copy in ins(i):
            copy.start()
    send[...] = jnp.zeros(send.shape, send.dtype)
    for copy in levels:
        copy.wait()
    ocean, ice, land = column(ocean_coef), column(ice_coef), column(land_coef)

    def body(step, _):
        for copy in ins(step):
            copy.wait()
        blocks = []
        for b in range(no + nl):
            is_ocean = b < no
            at = step * no + b if is_ocean else step * nl + b - no
            slots = [slot_ref[(0 if is_ocean else 2) + k, at] for k in range(2)]
            blocks.append((is_ocean, at, slots))
        for b, (is_ocean, at, slots) in enumerate(blocks):
            tiles = ot if is_ocean else lt
            src = jnp.concatenate([got_ref[s] for s in slots], axis=1)
            mixed[b] = near[step * (no + nl) + b] + dot(src, tiles[at].reshape(2 * BL, BL), NN)
        for b, (is_ocean, at, slots) in enumerate(blocks):
            u = mixed[b, pl.ds(0, 8, stride=3), :]
            v = mixed[b, pl.ds(1, 8, stride=3), :]
            t = mixed[b, pl.ds(2, 8, stride=3), :]
            wind = jnp.sqrt(1.0 + u * u + v * v)
            here = lanes(at)
            if is_ocean:
                frac = il[pl.ds(at, 1), :].astype(jnp.float32) / 8.0
                flux = (1.0 - frac) * (ocean * wind * (t - osv[:, here]))
                of[:, here] = flux + frac * (ice * wind * (t - isv[:, here]))
            else:
                frac = ll[pl.ds(at, 1), :].astype(jnp.float32) / 8.0
                lf[:, here] = frac * (land * wind * (t - ls[:, here]))
        for b, (is_ocean, at, slots) in enumerate(blocks):
            tiles, flux = (ot, of) if is_ocean else (lt, lf)
            g = flux[:, lanes(at)].astype(jnp.bfloat16)
            terms = dot(g, tiles[at].reshape(2 * BL, BL), NT).astype(send.dtype)
            for k in range(2):
                send[slots[k]] = terms[:, k * BL : (k + 1) * BL]
        return 0

    lax.fori_loop(0, STEPS, body, 0)
    outs = [
        pltpu.make_async_copy(a, b, out_sems.at[k])
        for k, (a, b) in enumerate(((send, send_hbm), (of, of_hbm), (lf, lf_hbm)))
    ]
    for copy in outs:
        copy.start()
    for copy in outs:
        copy.wait()


def far(slots, got, ot, lt, near, os, ice, il, ls, ll):
    ob, lb = ot.shape[0], lt.shape[0]
    nf, ns = near.shape[1], os.shape[0]
    f32 = jnp.float32
    back = (got.shape[0], ns, BL)
    return pl.pallas_call(
        far_kernel,
        out_shape=(
            jax.ShapeDtypeStruct(os.shape, f32),
            jax.ShapeDtypeStruct(ls.shape, f32),
            jax.ShapeDtypeStruct(back, jnp.bfloat16),
        ),
        in_specs=[whole(SMEM), *[whole(pl.ANY)] * 9],
        out_specs=[whole(pltpu.HBM)] * 3,
        scratch_shapes=[
            VMEM(got.shape, got.dtype),
            VMEM((ob, 2, BL, BL), ot.dtype),
            VMEM((lb, 2, BL, BL), lt.dtype),
            VMEM(near.shape, f32),
            VMEM(os.shape, f32),
            VMEM(ice.shape, f32),
            VMEM(il.shape, il.dtype),
            VMEM(ls.shape, f32),
            VMEM(ll.shape, ll.dtype),
            VMEM(os.shape, f32),
            VMEM(ls.shape, f32),
            VMEM(back, jnp.bfloat16),
            VMEM(((ob + lb) // STEPS, nf, BL), f32),
            pltpu.SemaphoreType.DMA((7, STEPS)),
            pltpu.SemaphoreType.DMA((3,)),
        ],
        compiler_params=pltpu.CompilerParams(vmem_limit_bytes=LARGE),
        name="far",
    )(slots, got, ot, lt, near, os, ice, il, ls, ll)


def near_back_kernel(ol_ref, ll_ref, of_ref, lf_ref, ot_ref, lt_ref, out_ref):
    step = pl.program_id(0)

    @pl.when(step == 0)
    def _():
        out_ref[...] = jnp.zeros(out_ref.shape, out_ref.dtype)

    for ids, flux, tiles in ((ol_ref, of_ref, ot_ref), (ll_ref, lf_ref, lt_ref)):
        n = tiles.shape[0]
        for b in range(n):
            g = flux[:, b * BL : (b + 1) * BL].astype(jnp.bfloat16)
            terms = dot(g, tiles[b].reshape(2 * BL, BL), NT)
            for k in range(2):
                at = lanes(ids[k, step * n + b])
                out_ref[:, at] = out_ref[:, at] + terms[:, k * BL : (k + 1) * BL]


def near_back(ol, ll, of, lf, ot, lt):
    ob, lb = ot.shape[0], lt.shape[0]
    ns = of.shape[0]
    return pl.pallas_call(
        near_back_kernel,
        grid=(STEPS,),
        out_shape=jax.ShapeDtypeStruct((ns, AB * BL), jnp.float32),
        in_specs=[
            whole(SMEM),
            whole(SMEM),
            pl.BlockSpec((ns, ob // STEPS * BL), lambda i: (0, i)),
            pl.BlockSpec((ns, lb // STEPS * BL), lambda i: (0, i)),
            *tile_specs(ob, lb, 1),
        ],
        out_specs=pl.BlockSpec((ns, AB * BL), lambda i: (0, 0)),
        compiler_params=pltpu.CompilerParams(vmem_limit_bytes=GRANT),
        cost_estimate=pl.CostEstimate(
            flops=2 * (ob + lb) * 2 * BL * BL * 128,
            bytes_accessed=(ob + lb) * 2 * BL * BL * 2,
            transcendentals=0,
        ),
        name="near_back",
    )(ol, ll, of, lf, ot, lt)


def collect_kernel(cells, neighbours, asked_ref, back_ref, *refs):
    if neighbours:
        out_ref, *totals = refs
    else:
        acc_ref, out_ref, acc, sem, *totals = refs
        load = pltpu.make_async_copy(acc_ref, acc, sem)
        load.start()
        totals = [acc, *totals]
    cell = lax.axis_index("cell")
    half = cells // 2
    for total in totals[-CHAINS:]:
        total[...] = jnp.zeros(total.shape, jnp.float32)

    def body(c, _):
        far_one = jnp.logical_or(c <= cell - half, c > cell + half)

        @pl.when(far_one == neighbours)
        def _():
            for r in range(CAP):
                total = totals[r % CHAINS - CHAINS]
                i = asked_ref[c, r]
                at = lanes(jnp.where(i < 0, AB, i & (AB - 1)))
                total[:, at] = total[:, at] + back_ref[c * CAP + r].astype(jnp.float32)

        return 0

    lax.fori_loop(0, cells, body, 0)
    if not neighbours:
        load.wait()
    for b in range(AB):
        here = slice(b * BL, (b + 1) * BL)
        out_ref[:, here] = functools.reduce(jnp.add, [ref[:, here] for ref in totals])


def collect(asked, back, acc, neighbours, cells):
    ns = back.shape[1]
    shape = (ns, AB * BL)
    accs, more = (), []
    if acc is not None:
        accs, more = (acc,), [VMEM(shape, jnp.float32), pltpu.SemaphoreType.DMA(())]
    return pl.pallas_call(
        functools.partial(collect_kernel, cells, neighbours),
        out_shape=jax.ShapeDtypeStruct(shape, jnp.float32),
        in_specs=[whole(SMEM), whole(), *[whole(pltpu.HBM)] * len(accs)],
        out_specs=whole(),
        scratch_shapes=[*more, *[VMEM((ns, (AB + 1) * BL), jnp.float32)] * CHAINS],
        compiler_params=pltpu.CompilerParams(vmem_limit_bytes=SMALL),
        cost_estimate=pl.CostEstimate(
            flops=1 << 20, bytes_accessed=4 << 20, transcendentals=0
        ),
        name="collect_far" if neighbours else "collect_own",
    )(asked, back, *accs)


def per_device(
    sects, cells, atm_fields, ocn_state, ice_state, ice_level, lnd_state, lnd_level,
    ocn_map, ocn_local, ocn_tiles, lnd_map, lnd_local, lnd_tiles,
):
    axes = ("sect", "cell")
    count = sects * cells
    half = cells // 2
    to_server = []
    for q in range(count):
        s, c = divmod(q, cells)
        to_server.append((q, (s + (1 if c >= half else -1)) % sects * cells + c))
    to_owner = [(b, a) for a, b in to_server]
    exchange = functools.partial(
        lax.all_to_all, axis_name="cell", split_axis=0, concat_axis=0, tiled=True
    )

    near_fields = lax.ppermute(atm_fields, axes, to_server)
    asking, slots = requests(ocn_map.T, lnd_map.T, cells)
    asked = exchange(asking)
    got = exchange(serve(asked, hold(atm_fields, near_fields), cells))
    ol, ll = ocn_local.T, lnd_local.T
    near = near_mix(ol, ll, atm_fields, ocn_tiles, lnd_tiles)
    of, lf, send = far(
        slots, got, ocn_tiles, lnd_tiles, near, ocn_state, ice_state,
        ice_level.reshape(-1, BL), lnd_state, lnd_level.reshape(-1, BL),
    )
    back = exchange(send)
    acc = near_back(ol, ll, of, lf, ocn_tiles, lnd_tiles)
    back, acc = lax.optimization_barrier((back, acc))
    away = lax.ppermute(collect(asked, back, None, True, cells), axes, to_owner)
    own = collect(asked, back, acc, False, cells)
    return own + away, of, lf


def solution(mesh):
    a = ("sect", "cell")
    in_specs = (
        P(None, a), P(None, a), P(None, a), P(a), P(None, a), P(a),
        P(a, None), P(a, None), P(a, None, None, None),
        P(a, None), P(a, None), P(a, None, None, None),
    )
    return jax.shard_map(
        functools.partial(per_device, mesh.shape["sect"], mesh.shape["cell"]),
        mesh=mesh,
        in_specs=in_specs,
        out_specs=(P(None, a), P(None, a), P(None, a)),
        check_vma=False,
    )
```

```python
import functools

import jax
import jax.numpy as jnp
from jax import lax
from jax.experimental import pallas as pl
from jax.experimental.pallas import tpu as pltpu
from jax.sharding import PartitionSpec as P

ocean_coef = (1.2, 0.9, 1.5, 0.7, 1.1, 1.3, 0.8, 1.0)
ice_coef = (0.5, 1.4, 0.6, 1.2, 0.9, 0.4, 1.6, 0.7)
land_coef = (0.8, 1.1, 0.6, 1.5, 0.7, 1.2, 1.0, 0.5)

BL = 128
AB = 32
KR = KL = 2
CAP = 15
GRANT, LARGE, SMALL = 60 << 20, 50 << 20, 8 << 20
CHAINS = 5
VMEM = pltpu.VMEM
SMEM = pltpu.SMEM
NN = (((1,), (0,)), ((), ()))
NT = (((1,), (1,)), ((), ()))


def dot(a, b, dims):
    return lax.dot_general(a, b, dims, preferred_element_type=jnp.float32)


def lanes(i):
    return pl.ds(pl.multiple_of(i * BL, BL), BL)


def whole(space=VMEM):
    return pl.BlockSpec(memory_space=space)


def column(values, width):
    row = lax.broadcasted_iota(jnp.int32, (8, BL), 0)
    out = jnp.full((8, BL), values[7], jnp.float32)
    for j in range(7):
        out = jnp.where(row == j, values[j], out)
    return jnp.concatenate([out] * (width // BL), axis=1)


def request_kernel(cells, om_ref, lm_ref, req_ref, slot_ref):
    sect = lax.axis_index("sect")
    before = jnp.zeros((cells, 1), jnp.float32)
    req = jnp.zeros((cells, BL), jnp.float32)
    slot_ref[...] = jnp.zeros(slot_ref.shape, jnp.int32)
    row = 0
    for ref in (om_ref, lm_ref):
        n = ref.shape[1]
        earlier = lax.broadcasted_iota(jnp.int32, (n, n), 0) < lax.broadcasted_iota(
            jnp.int32, (n, n), 1
        )
        earlier = jnp.where(earlier, 1.0, 0.0).astype(jnp.bfloat16)
        for k in range(ref.shape[0]):
            src = ref[k : k + 1, :]
            owner = src // AB
            col = owner % cells
            value = src % AB + jnp.where(owner // cells == sect, 0, AB)
            chosen = lax.broadcasted_iota(jnp.int32, (cells, n), 0) == col
            onehot = jnp.where(chosen, 1.0, 0.0)
            ranks = before + dot(onehot.astype(jnp.bfloat16), earlier, NN)
            rank = jnp.sum(jnp.where(chosen, ranks, 0.0), axis=0, keepdims=True)
            before = before + jnp.sum(onehot, axis=1, keepdims=True)
            place = lax.broadcasted_iota(jnp.int32, (BL, n), 0) == rank.astype(jnp.int32)
            place = jnp.where(place, 1.0, 0.0).astype(jnp.bfloat16)
            asked = jnp.where(chosen, (value + 1).astype(jnp.float32), 0.0)
            req = req + dot(asked.astype(jnp.bfloat16), place, NT)
            slot_ref[row : row + 1, :n] = col * CAP + rank.astype(jnp.int32)
            row += 1
    req_ref[...] = req.astype(jnp.int32) - 1


def requests(om, lm, cells):
    return pl.pallas_call(
        functools.partial(request_kernel, cells),
        out_shape=(
            jax.ShapeDtypeStruct((cells, BL), jnp.int32),
            jax.ShapeDtypeStruct((8, BL), jnp.int32),
        ),
        in_specs=[whole()] * 2,
        out_specs=[whole()] * 2,
        compiler_params=pltpu.CompilerParams(vmem_limit_bytes=GRANT),
        name="requests",
    )(om, lm)


def hold_kernel(own_ref, near_ref, out_ref):
    nf, width = own_ref.shape
    rows = lax.broadcasted_iota(jnp.int32, (nf, nf), 0)
    pick = 3 * (rows % 8) + rows // 8 == lax.broadcasted_iota(jnp.int32, (nf, nf), 1)
    pick = jnp.where(pick, 1.0, 0.0).astype(own_ref.dtype)
    for k, ref in enumerate((own_ref, near_ref)):
        for at in range(0, width, 8 * BL):
            part = dot(pick, ref[:, at : at + 8 * BL], NN)
            out_ref[:, k * width + at : k * width + at + 8 * BL] = part.astype(out_ref.dtype)


def hold(own, near):
    return pl.pallas_call(
        hold_kernel,
        out_shape=jax.ShapeDtypeStruct((own.shape[0], 2 * own.shape[1]), own.dtype),
        in_specs=[whole()] * 2,
        out_specs=whole(),
        compiler_params=pltpu.CompilerParams(vmem_limit_bytes=SMALL),
        cost_estimate=pl.CostEstimate(flops=1 << 20, bytes_accessed=4 << 20, transcendentals=0),
        name="hold",
    )(own, near)


def serve_kernel(cells, asked_ref, both, out_ref, made, out_sems):
    def out(c):
        part = pl.ds(c * CAP, CAP)
        return pltpu.make_async_copy(made.at[part], out_ref.at[part], out_sems.at[c])

    def body(c, _):
        for r in range(CAP):
            i = jnp.maximum(asked_ref[c, r], 0)
            made[c * CAP + r] = both[:, lanes(i)]
        out(c).start()
        return 0

    lax.fori_loop(0, cells, body, 0)
    for c in range(cells):
        out(c).wait()


def serve(asked, both, cells):
    shape = (cells * CAP, both.shape[0], BL)
    return pl.pallas_call(
        functools.partial(serve_kernel, cells),
        out_shape=jax.ShapeDtypeStruct(shape, both.dtype),
        in_specs=[whole(SMEM), whole()],
        out_specs=whole(pltpu.HBM),
        scratch_shapes=[VMEM(shape, both.dtype), pltpu.SemaphoreType.DMA((cells,))],
        compiler_params=pltpu.CompilerParams(vmem_limit_bytes=SMALL),
        name="serve",
    )(asked, both)


STEPS = 4
OPARTS, LPARTS = (0, 2, 6, 11, 16), (0, 16)


def tile_specs(ob, lb, half):
    return [
        pl.BlockSpec((ob // STEPS, 2, BL, BL), lambda i: (i, half, 0, 0)),
        pl.BlockSpec((lb // STEPS, 2, BL, BL), lambda i: (i, half, 0, 0)),
    ]


def near_mix_kernel(ol_ref, ll_ref, f_ref, ot_ref, lt_ref, out_ref):
    step = pl.program_id(0)
    at = 0
    for ids, tiles in ((ol_ref, ot_ref), (ll_ref, lt_ref)):
        n = tiles.shape[0]
        for b in range(n):
            src = [f_ref[:, lanes(ids[k, step * n + b])] for k in range(2)]
            out_ref[at] = dot(
                jnp.concatenate(src, axis=1), tiles[b].reshape(2 * BL, BL), NN
            )
            at += 1


def near_mix(ol, ll, fields, ot, lt):
    ob, lb = ot.shape[0], lt.shape[0]
    nf = fields.shape[0]
    return pl.pallas_call(
        near_mix_kernel,
        grid=(STEPS,),
        out_shape=jax.ShapeDtypeStruct((ob + lb, nf, BL), jnp.float32),
        in_specs=[
            whole(SMEM),
            whole(SMEM),
            pl.BlockSpec(fields.shape, lambda i: (0, 0)),
            *tile_specs(ob, lb, 1),
        ],
        out_specs=pl.BlockSpec(((ob + lb) // STEPS, nf, BL), lambda i: (i, 0, 0)),
        compiler_params=pltpu.CompilerParams(vmem_limit_bytes=52 << 20),
        cost_estimate=pl.CostEstimate(
            flops=2 * (ob + lb) * 2 * BL * BL * 128,
            bytes_accessed=(ob + lb) * 2 * BL * BL * 2,
            transcendentals=0,
        ),
        name="near_mix",
    )(ol, ll, fields, ot, lt)


def portions(count, parts):
    cuts = [count * p // 16 for p in parts]
    return list(zip(cuts[:-1], cuts[1:]))


def far_kernel(
    slot_ref, got_ref, near, osv, isv, il, ls, ll, ot_hbm, lt_hbm, of_hbm, lf_hbm, send_hbm,
    ot, lt, of, lf, send, in_sems, out_sems,
):
    ob, lb = ot.shape[0], lt.shape[0]
    parts = [(0, *p) for p in portions(ob, OPARTS)] + [(1, *p) for p in portions(lb, LPARTS)]
    ins, outs = [], []
    for i, (kind, lo, hi) in enumerate(parts):
        hbm, on_chip = (lt_hbm, lt) if kind else (ot_hbm, ot)
        some = pl.ds(lo, hi - lo)
        copy = pltpu.make_async_copy(
            hbm.at[some, pl.ds(0, KR)], on_chip.at[some], in_sems.at[i]
        )
        copy.start()
        ins.append(copy)
        flux, flux_hbm = (lf, lf_hbm) if kind else (of, of_hbm)
        some = pl.ds(lo * BL, (hi - lo) * BL)
        outs.append(
            pltpu.make_async_copy(flux.at[:, some], flux_hbm.at[:, some], out_sems.at[i])
        )
    send[...] = jnp.zeros(send.shape, send.dtype)
    for i, (kind, lo, hi) in enumerate(parts):
        ins[i].wait()
        few, n = range(lo, hi), hi - lo
        tiles = lt if kind else ot
        slots = [[slot_ref[2 * kind + k, b] for k in range(KR)] for b in few]
        weights = [tiles[b].reshape(KR * BL, BL) for b in few]
        no, nl = ob // STEPS, lb // STEPS
        at = [
            (b // nl) * (no + nl) + no + b % nl if kind else (b // no) * (no + nl) + b % no
            for b in few
        ]
        rows = []
        for j in range(n):
            source = jnp.concatenate([got_ref[s] for s in slots[j]], axis=1)
            rows.append(near[at[j]] + dot(source, weights[j], NN))
        u, v, t = (
            jnp.concatenate([row[8 * j : 8 * j + 8] for row in rows], axis=1) for j in range(3)
        )
        wind = jnp.sqrt(1.0 + u * u + v * v)
        here = slice(lo * BL, hi * BL)
        level = (ll if kind else il)[lo:hi, :].astype(jnp.float32) * 0.125
        level = [jnp.broadcast_to(level[j : j + 1], (8, BL)) for j in range(n)]
        frac = jnp.concatenate(level, axis=1)

        def bulk(factors, state):
            return column(factors, n * BL) * wind * (t - state[:, here])

        if kind:
            flux = frac * bulk(land_coef, ls)
            lf[:, here] = flux
        else:
            flux = (1.0 - frac) * bulk(ocean_coef, osv) + frac * bulk(ice_coef, isv)
            of[:, here] = flux
        outs[i].start()
        flux = flux.astype(jnp.bfloat16)
        for j in range(n):
            terms = dot(flux[:, j * BL : (j + 1) * BL], weights[j], NT).astype(send.dtype)
            for k in range(KR):
                send[slots[j][k]] = terms[:, k * BL : (k + 1) * BL]
    outs.append(pltpu.make_async_copy(send, send_hbm, out_sems.at[len(parts)]))
    outs[-1].start()
    for copy in outs:
        copy.wait()


def far(slots, got, near, os, ice, il, ls, ll, ot, lt):
    f32 = jnp.float32
    back = (got.shape[0], os.shape[0], BL)
    count = len(OPARTS) + len(LPARTS) - 2
    return pl.pallas_call(
        far_kernel,
        out_shape=(
            jax.ShapeDtypeStruct(os.shape, f32),
            jax.ShapeDtypeStruct(ls.shape, f32),
            jax.ShapeDtypeStruct(back, jnp.bfloat16),
        ),
        in_specs=[whole(SMEM), *[whole()] * 7, *[whole(pl.ANY)] * 2],
        out_specs=[whole(pltpu.HBM)] * 3,
        scratch_shapes=[
            VMEM((ot.shape[0], KR, BL, BL), ot.dtype),
            VMEM((lt.shape[0], KR, BL, BL), lt.dtype),
            VMEM(os.shape, f32),
            VMEM(ls.shape, f32),
            VMEM(back, jnp.bfloat16),
            pltpu.SemaphoreType.DMA((count,)),
            pltpu.SemaphoreType.DMA((count + 1,)),
        ],
        compiler_params=pltpu.CompilerParams(vmem_limit_bytes=50 << 20),
        name="far",
    )(slots, got, near, os, ice, il, ls, ll, ot, lt)


def near_back_kernel(ol_ref, ll_ref, of_ref, lf_ref, ot_ref, lt_ref, out_ref):
    step = pl.program_id(0)

    @pl.when(step == 0)
    def _():
        out_ref[...] = jnp.zeros(out_ref.shape, out_ref.dtype)

    for ids, flux, tiles in ((ol_ref, of_ref, ot_ref), (ll_ref, lf_ref, lt_ref)):
        n = tiles.shape[0]
        for b in range(n):
            g = flux[:, b * BL : (b + 1) * BL].astype(jnp.bfloat16)
            terms = dot(g, tiles[b].reshape(2 * BL, BL), NT)
            for k in range(2):
                at = lanes(ids[k, step * n + b])
                out_ref[:, at] = out_ref[:, at] + terms[:, k * BL : (k + 1) * BL]


def near_back(ol, ll, of, lf, ot, lt):
    ob, lb = ot.shape[0], lt.shape[0]
    ns = of.shape[0]
    return pl.pallas_call(
        near_back_kernel,
        grid=(STEPS,),
        out_shape=jax.ShapeDtypeStruct((ns, AB * BL), jnp.float32),
        in_specs=[
            whole(SMEM),
            whole(SMEM),
            pl.BlockSpec((ns, ob // STEPS * BL), lambda i: (0, i)),
            pl.BlockSpec((ns, lb // STEPS * BL), lambda i: (0, i)),
            *tile_specs(ob, lb, 1),
        ],
        out_specs=pl.BlockSpec((ns, AB * BL), lambda i: (0, 0)),
        compiler_params=pltpu.CompilerParams(vmem_limit_bytes=GRANT),
        cost_estimate=pl.CostEstimate(
            flops=2 * (ob + lb) * 2 * BL * BL * 128,
            bytes_accessed=(ob + lb) * 2 * BL * BL * 2,
            transcendentals=0,
        ),
        name="near_back",
    )(ol, ll, of, lf, ot, lt)


def collect_kernel(cells, neighbours, asked_ref, back_ref, *refs):
    if neighbours:
        out_ref, *totals = refs
    else:
        acc_ref, out_ref, acc, sem, *totals = refs
        load = pltpu.make_async_copy(acc_ref, acc, sem)
        load.start()
        totals = [acc, *totals]
    cell = lax.axis_index("cell")
    half = cells // 2
    for total in totals[-CHAINS:]:
        total[...] = jnp.zeros(total.shape, jnp.float32)

    def body(c, _):
        far_one = jnp.logical_or(c <= cell - half, c > cell + half)

        @pl.when(far_one == neighbours)
        def _():
            for r in range(CAP):
                total = totals[r % CHAINS - CHAINS]
                i = asked_ref[c, r]
                at = lanes(jnp.where(i < 0, AB, i & (AB - 1)))
                total[:, at] = total[:, at] + back_ref[c * CAP + r].astype(jnp.float32)

        return 0

    lax.fori_loop(0, cells, body, 0)
    if not neighbours:
        load.wait()
    for b in range(AB):
        here = slice(b * BL, (b + 1) * BL)
        out_ref[:, here] = functools.reduce(jnp.add, [ref[:, here] for ref in totals])


def collect(asked, back, acc, neighbours, cells):
    ns = back.shape[1]
    shape = (ns, AB * BL)
    accs, more = (), []
    if acc is not None:
        accs, more = (acc,), [VMEM(shape, jnp.float32), pltpu.SemaphoreType.DMA(())]
    return pl.pallas_call(
        functools.partial(collect_kernel, cells, neighbours),
        out_shape=jax.ShapeDtypeStruct(shape, jnp.float32),
        in_specs=[whole(SMEM), whole(), *[whole(pltpu.HBM)] * len(accs)],
        out_specs=whole(),
        scratch_shapes=[*more, *[VMEM((ns, (AB + 1) * BL), jnp.float32)] * CHAINS],
        compiler_params=pltpu.CompilerParams(vmem_limit_bytes=SMALL),
        cost_estimate=pl.CostEstimate(
            flops=1 << 20, bytes_accessed=4 << 20, transcendentals=0
        ),
        name="collect_far" if neighbours else "collect_own",
    )(asked, back, *accs)


def per_device(
    sects, cells, atm_fields, ocn_state, ice_state, ice_level, lnd_state, lnd_level,
    ocn_map, ocn_local, ocn_tiles, lnd_map, lnd_local, lnd_tiles,
):
    axes = ("sect", "cell")
    count = sects * cells
    half = cells // 2
    to_server = []
    for q in range(count):
        s, c = divmod(q, cells)
        to_server.append((q, (s + (1 if c >= half else -1)) % sects * cells + c))
    to_owner = [(b, a) for a, b in to_server]
    exchange = functools.partial(
        lax.all_to_all, axis_name="cell", split_axis=0, concat_axis=0, tiled=True
    )

    near_fields = lax.ppermute(atm_fields, axes, to_server)
    asking, slots = requests(ocn_map.T, lnd_map.T, cells)
    asked = exchange(asking)
    held = hold(atm_fields, near_fields)
    got = exchange(serve(asked, held, cells))
    ol, ll = ocn_local.T, lnd_local.T
    near = near_mix(ol, ll, held, ocn_tiles, lnd_tiles)
    of, lf, send = far(
        slots, got, near, ocn_state, ice_state, ice_level.reshape(-1, BL), lnd_state,
        lnd_level.reshape(-1, BL), ocn_tiles, lnd_tiles,
    )
    back = exchange(send)
    acc = near_back(ol, ll, of, lf, ocn_tiles, lnd_tiles)
    back, acc = lax.optimization_barrier((back, acc))
    away = lax.ppermute(collect(asked, back, None, True, cells), axes, to_owner)
    own = collect(asked, back, acc, False, cells)
    return own + away, of, lf


def solution(mesh):
    a = ("sect", "cell")
    in_specs = (
        P(None, a), P(None, a), P(None, a), P(a), P(None, a), P(a),
        P(a, None), P(a, None), P(a, None, None, None),
        P(a, None), P(a, None), P(a, None, None, None),
    )
    return jax.shard_map(
        functools.partial(per_device, mesh.shape["sect"], mesh.shape["cell"]),
        mesh=mesh,
        in_specs=in_specs,
        out_specs=(P(None, a), P(None, a), P(None, a)),
        check_vma=False,
    )
```

```python
import functools

import jax
import jax.numpy as jnp
from jax import lax
from jax.experimental import pallas as pl
from jax.experimental.pallas import tpu as pltpu
from jax.sharding import PartitionSpec as P

ocean_coef = (1.2, 0.9, 1.5, 0.7, 1.1, 1.3, 0.8, 1.0)
ice_coef = (0.5, 1.4, 0.6, 1.2, 0.9, 0.4, 1.6, 0.7)
land_coef = (0.8, 1.1, 0.6, 1.5, 0.7, 1.2, 1.0, 0.5)

BL = 128
AB_BITS = 5
AB = 1 << AB_BITS
KR = KL = 2
CAP = 15
GRANT, LARGE, SMALL = 60 << 20, 50 << 20, 8 << 20
CHAINS = 5
VMEM = pltpu.VMEM
SMEM = pltpu.SMEM
NN = (((1,), (0,)), ((), ()))
NT = (((1,), (1,)), ((), ()))


def dot(a, b, dims):
    return lax.dot_general(a, b, dims, preferred_element_type=jnp.float32)


def lanes(i):
    return pl.ds(pl.multiple_of(i * BL, BL), BL)


def whole(space=VMEM):
    return pl.BlockSpec(memory_space=space)


def column(values, width):
    row = lax.broadcasted_iota(jnp.int32, (8, BL), 0)
    out = jnp.full((8, BL), values[7], jnp.float32)
    for j in range(7):
        out = jnp.where(row == j, values[j], out)
    return jnp.concatenate([out] * (width // BL), axis=1)


def request_kernel(cells, om_ref, lm_ref, req_ref, slot_ref):
    sect = lax.axis_index("sect")
    cell_bits = cells.bit_length() - 1
    before = jnp.zeros((cells, 1), jnp.float32)
    req = jnp.zeros((cells, BL), jnp.float32)
    slot_ref[...] = jnp.zeros(slot_ref.shape, jnp.int32)
    row = 0
    for ref in (om_ref, lm_ref):
        n = ref.shape[1]
        earlier = lax.broadcasted_iota(jnp.int32, (n, n), 0) < lax.broadcasted_iota(
            jnp.int32, (n, n), 1
        )
        earlier = jnp.where(earlier, 1.0, 0.0).astype(jnp.bfloat16)
        for k in range(ref.shape[0]):
            src = ref[k : k + 1, :]
            owner = src >> AB_BITS
            col = owner & (cells - 1)
            value = (src & (AB - 1)) + jnp.where(owner >> cell_bits == sect, 0, AB)
            chosen = lax.broadcasted_iota(jnp.int32, (cells, n), 0) == col
            onehot = jnp.where(chosen, 1.0, 0.0)
            ranks = before + dot(onehot.astype(jnp.bfloat16), earlier, NN)
            rank = jnp.sum(jnp.where(chosen, ranks, 0.0), axis=0, keepdims=True)
            before = before + jnp.sum(onehot, axis=1, keepdims=True)
            place = lax.broadcasted_iota(jnp.int32, (BL, n), 0) == rank.astype(jnp.int32)
            place = jnp.where(place, 1.0, 0.0).astype(jnp.bfloat16)
            asked = jnp.where(chosen, (value + 1).astype(jnp.float32), 0.0)
            req = req + dot(asked.astype(jnp.bfloat16), place, NT)
            slot_ref[row : row + 1, :n] = col * CAP + rank.astype(jnp.int32)
            row += 1
    req_ref[...] = req.astype(jnp.int32) - 1


def requests(om, lm, cells):
    return pl.pallas_call(
        functools.partial(request_kernel, cells),
        out_shape=(
            jax.ShapeDtypeStruct((cells, BL), jnp.int32),
            jax.ShapeDtypeStruct((8, BL), jnp.int32),
        ),
        in_specs=[whole()] * 2,
        out_specs=[whole()] * 2,
        compiler_params=pltpu.CompilerParams(vmem_limit_bytes=GRANT),
        name="requests",
    )(om, lm)


def hold_kernel(own_ref, near_ref, out_ref):
    nf, width = own_ref.shape
    rows = lax.broadcasted_iota(jnp.int32, (nf, nf), 0)
    pick = 3 * (rows & 7) + (rows >> 3) == lax.broadcasted_iota(jnp.int32, (nf, nf), 1)
    pick = jnp.where(pick, 1.0, 0.0).astype(own_ref.dtype)
    for k, ref in enumerate((own_ref, near_ref)):
        for at in range(0, width, 8 * BL):
            part = dot(pick, ref[:, at : at + 8 * BL], NN)
            out_ref[:, k * width + at : k * width + at + 8 * BL] = part.astype(out_ref.dtype)


def hold(own, near):
    return pl.pallas_call(
        hold_kernel,
        out_shape=jax.ShapeDtypeStruct((own.shape[0], 2 * own.shape[1]), own.dtype),
        in_specs=[whole()] * 2,
        out_specs=whole(),
        compiler_params=pltpu.CompilerParams(vmem_limit_bytes=SMALL),
        cost_estimate=pl.CostEstimate(flops=1 << 20, bytes_accessed=4 << 20, transcendentals=0),
        name="hold",
    )(own, near)


def serve_kernel(cells, asked_ref, both, out_ref, made, out_sems):
    def out(c):
        part = pl.ds(c * CAP, CAP)
        return pltpu.make_async_copy(made.at[part], out_ref.at[part], out_sems.at[c])

    def body(c, _):
        for r in range(CAP):
            i = jnp.maximum(asked_ref[c, r], 0)
            made[c * CAP + r] = both[:, lanes(i)]
        out(c).start()
        return 0

    lax.fori_loop(0, cells, body, 0)
    for c in range(cells):
        out(c).wait()


def serve(asked, both, cells):
    shape = (cells * CAP, both.shape[0], BL)
    return pl.pallas_call(
        functools.partial(serve_kernel, cells),
        out_shape=jax.ShapeDtypeStruct(shape, both.dtype),
        in_specs=[whole(SMEM), whole()],
        out_specs=whole(pltpu.HBM),
        scratch_shapes=[VMEM(shape, both.dtype), pltpu.SemaphoreType.DMA((cells,))],
        compiler_params=pltpu.CompilerParams(vmem_limit_bytes=SMALL),
        name="serve",
    )(asked, both)


STEPS = 4
OPARTS, LPARTS = (0, 2, 6, 11, 16), (0, 16)


def tile_specs(ob, lb, half):
    return [
        pl.BlockSpec((ob // STEPS, 2, BL, BL), lambda i: (i, half, 0, 0)),
        pl.BlockSpec((lb // STEPS, 2, BL, BL), lambda i: (i, half, 0, 0)),
    ]


def near_mix_kernel(ol_ref, ll_ref, f_ref, ot_ref, lt_ref, lt_hbm, out_ref, bring_ref, sem):
    step = pl.program_id(0)
    bring = pltpu.make_async_copy(lt_hbm.at[:, pl.ds(0, KR)], bring_ref, sem)

    @pl.when(step == 0)
    def _():
        bring.start()

    at = 0
    for ids, tiles in ((ol_ref, ot_ref), (ll_ref, lt_ref)):
        n = tiles.shape[0]
        for b in range(n):
            src = [f_ref[:, lanes(ids[k, step * n + b])] for k in range(2)]
            out_ref[at] = dot(
                jnp.concatenate(src, axis=1), tiles[b].reshape(2 * BL, BL), NN
            )
            at += 1

    @pl.when(step == STEPS - 1)
    def _():
        bring.wait()


def near_mix(ol, ll, fields, ot, lt):
    ob, lb = ot.shape[0], lt.shape[0]
    nf = fields.shape[0]
    return pl.pallas_call(
        near_mix_kernel,
        grid=(STEPS,),
        out_shape=(
            jax.ShapeDtypeStruct((ob + lb, nf, BL), jnp.float32),
            jax.ShapeDtypeStruct((lb, KR, BL, BL), lt.dtype),
        ),
        in_specs=[
            whole(SMEM),
            whole(SMEM),
            pl.BlockSpec(fields.shape, lambda i: (0, 0)),
            *tile_specs(ob, lb, 1),
            whole(pl.ANY),
        ],
        out_specs=[
            pl.BlockSpec(((ob + lb) // STEPS, nf, BL), lambda i: (i, 0, 0)),
            whole(),
        ],
        scratch_shapes=[pltpu.SemaphoreType.DMA(())],
        compiler_params=pltpu.CompilerParams(vmem_limit_bytes=51 << 20),
        cost_estimate=pl.CostEstimate(
            flops=2 * (ob + lb) * 2 * BL * BL * 128,
            bytes_accessed=(ob + lb) * 2 * BL * BL * 2,
            transcendentals=0,
        ),
        name="near_mix",
    )(ol, ll, fields, ot, lt, lt)


def portions(count, parts):
    cuts = [count * p // 16 for p in parts]
    return list(zip(cuts[:-1], cuts[1:]))


def far_kernel(
    slot_ref, got_ref, near, osv, isv, il, ls, ll, lt, ot_hbm, of_hbm, lf_hbm, send_hbm,
    ot, of, lf, send, in_sems, out_sems,
):
    ob, lb = ot.shape[0], lt.shape[0]
    parts = [(1, *p) for p in portions(lb, LPARTS)] + [(0, *p) for p in portions(ob, OPARTS)]
    ins, outs = [], []
    for i, (kind, lo, hi) in enumerate(parts):
        some = pl.ds(lo, hi - lo)
        if not kind:
            copy = pltpu.make_async_copy(
                ot_hbm.at[some, pl.ds(0, KR)], ot.at[some], in_sems.at[i]
            )
            copy.start()
        ins.append(None if kind else copy)
        flux, flux_hbm = (lf, lf_hbm) if kind else (of, of_hbm)
        some = pl.ds(lo * BL, (hi - lo) * BL)
        outs.append(
            pltpu.make_async_copy(flux.at[:, some], flux_hbm.at[:, some], out_sems.at[i])
        )
    send[...] = jnp.zeros(send.shape, send.dtype)
    for i, (kind, lo, hi) in enumerate(parts):
        if not kind:
            ins[i].wait()
        few, n = range(lo, hi), hi - lo
        tiles = lt if kind else ot
        slots = [[slot_ref[2 * kind + k, b] for k in range(KR)] for b in few]
        weights = [tiles[b].reshape(KR * BL, BL) for b in few]
        no, nl = ob // STEPS, lb // STEPS
        at = [
            (b // nl) * (no + nl) + no + b % nl if kind else (b // no) * (no + nl) + b % no
            for b in few
        ]
        rows = []
        for j in range(n):
            source = jnp.concatenate([got_ref[s] for s in slots[j]], axis=1)
            rows.append(near[at[j]] + dot(source, weights[j], NN))
        u, v, t = (
            jnp.concatenate([row[8 * j : 8 * j + 8] for row in rows], axis=1) for j in range(3)
        )
        wind = jnp.sqrt(1.0 + u * u + v * v)
        here = slice(lo * BL, hi * BL)
        level = (ll if kind else il)[lo:hi, :].astype(jnp.float32) * 0.125
        level = [jnp.broadcast_to(level[j : j + 1], (8, BL)) for j in range(n)]
        frac = jnp.concatenate(level, axis=1)

        def bulk(factors, state):
            return column(factors, n * BL) * wind * (t - state[:, here])

        if kind:
            flux = frac * bulk(land_coef, ls)
            lf[:, here] = flux
        else:
            flux = (1.0 - frac) * bulk(ocean_coef, osv) + frac * bulk(ice_coef, isv)
            of[:, here] = flux
        outs[i].start()
        flux = flux.astype(jnp.bfloat16)
        for j in range(n):
            terms = dot(flux[:, j * BL : (j + 1) * BL], weights[j], NT).astype(send.dtype)
            for k in range(KR):
                send[slots[j][k]] = terms[:, k * BL : (k + 1) * BL]
    outs.append(pltpu.make_async_copy(send, send_hbm, out_sems.at[len(parts)]))
    outs[-1].start()
    for copy in outs:
        copy.wait()


def far(slots, got, near, os, ice, il, ls, ll, lt, ot):
    f32 = jnp.float32
    back = (got.shape[0], os.shape[0], BL)
    count = len(OPARTS) + len(LPARTS) - 2
    return pl.pallas_call(
        far_kernel,
        out_shape=(
            jax.ShapeDtypeStruct(os.shape, f32),
            jax.ShapeDtypeStruct(ls.shape, f32),
            jax.ShapeDtypeStruct(back, jnp.bfloat16),
        ),
        in_specs=[whole(SMEM), *[whole()] * 8, whole(pl.ANY)],
        out_specs=[whole(pltpu.HBM)] * 3,
        scratch_shapes=[
            VMEM((ot.shape[0], KR, BL, BL), ot.dtype),
            VMEM(os.shape, f32),
            VMEM(ls.shape, f32),
            VMEM(back, jnp.bfloat16),
            pltpu.SemaphoreType.DMA((count,)),
            pltpu.SemaphoreType.DMA((count + 1,)),
        ],
        compiler_params=pltpu.CompilerParams(vmem_limit_bytes=50 << 20),
        name="far",
    )(slots, got, near, os, ice, il, ls, ll, lt, ot)


def near_back_kernel(ol_ref, ll_ref, of_ref, lf_ref, ot_ref, lt_ref, out_ref):
    step = pl.program_id(0)

    @pl.when(step == 0)
    def _():
        out_ref[...] = jnp.zeros(out_ref.shape, out_ref.dtype)

    for ids, flux, tiles in ((ol_ref, of_ref, ot_ref), (ll_ref, lf_ref, lt_ref)):
        n = tiles.shape[0]
        for b in range(n):
            g = flux[:, b * BL : (b + 1) * BL].astype(jnp.bfloat16)
            terms = dot(g, tiles[b].reshape(2 * BL, BL), NT)
            for k in range(2):
                at = lanes(ids[k, step * n + b])
                out_ref[:, at] = out_ref[:, at] + terms[:, k * BL : (k + 1) * BL]


def near_back(ol, ll, of, lf, ot, lt):
    ob, lb = ot.shape[0], lt.shape[0]
    ns = of.shape[0]
    return pl.pallas_call(
        near_back_kernel,
        grid=(STEPS,),
        out_shape=jax.ShapeDtypeStruct((ns, AB * BL), jnp.float32),
        in_specs=[
            whole(SMEM),
            whole(SMEM),
            pl.BlockSpec((ns, ob // STEPS * BL), lambda i: (0, i)),
            pl.BlockSpec((ns, lb // STEPS * BL), lambda i: (0, i)),
            *tile_specs(ob, lb, 1),
        ],
        out_specs=pl.BlockSpec((ns, AB * BL), lambda i: (0, 0)),
        compiler_params=pltpu.CompilerParams(vmem_limit_bytes=GRANT),
        cost_estimate=pl.CostEstimate(
            flops=2 * (ob + lb) * 2 * BL * BL * 128,
            bytes_accessed=(ob + lb) * 2 * BL * BL * 2,
            transcendentals=0,
        ),
        name="near_back",
    )(ol, ll, of, lf, ot, lt)


def collect_kernel(cells, neighbours, asked_ref, back_ref, *refs):
    if neighbours:
        out_ref, *totals = refs
    else:
        acc_ref, out_ref, acc, sem, *totals = refs
        load = pltpu.make_async_copy(acc_ref, acc, sem)
        load.start()
        totals = [acc, *totals]
    cell = lax.axis_index("cell")
    half = cells // 2
    for total in totals[-CHAINS:]:
        total[...] = jnp.zeros(total.shape, jnp.float32)

    def body(c, _):
        far_one = jnp.logical_or(c <= cell - half, c > cell + half)

        @pl.when(far_one == neighbours)
        def _():
            for r in range(CAP):
                total = totals[r % CHAINS - CHAINS]
                i = asked_ref[c, r]
                at = lanes(jnp.where(i < 0, AB, i & (AB - 1)))
                total[:, at] = total[:, at] + back_ref[c * CAP + r].astype(jnp.float32)

        return 0

    lax.fori_loop(0, cells, body, 0)
    if not neighbours:
        load.wait()
    for b in range(AB):
        here = slice(b * BL, (b + 1) * BL)
        total = functools.reduce(jnp.add, [ref[:, here] for ref in totals])
        out_ref[:, here] = total.astype(out_ref.dtype)


def collect(asked, back, acc, neighbours, cells):
    ns = back.shape[1]
    shape = (ns, AB * BL)
    accs, more = (), []
    if acc is not None:
        accs, more = (acc,), [VMEM(shape, jnp.float32), pltpu.SemaphoreType.DMA(())]
    return pl.pallas_call(
        functools.partial(collect_kernel, cells, neighbours),
        out_shape=jax.ShapeDtypeStruct(shape, jnp.float32 if accs else back.dtype),
        in_specs=[whole(SMEM), whole(), *[whole(pltpu.HBM)] * len(accs)],
        out_specs=whole(),
        scratch_shapes=[*more, *[VMEM((ns, (AB + 1) * BL), jnp.float32)] * CHAINS],
        compiler_params=pltpu.CompilerParams(vmem_limit_bytes=SMALL),
        cost_estimate=pl.CostEstimate(
            flops=1 << 20, bytes_accessed=4 << 20, transcendentals=0
        ),
        name="collect_far" if neighbours else "collect_own",
    )(asked, back, *accs)


def per_device(
    sects, cells, atm_fields, ocn_state, ice_state, ice_level, lnd_state, lnd_level,
    ocn_map, ocn_local, ocn_tiles, lnd_map, lnd_local, lnd_tiles,
):
    axes = ("sect", "cell")
    count = sects * cells
    half = cells // 2
    to_server = []
    for q in range(count):
        s, c = divmod(q, cells)
        to_server.append((q, (s + (1 if c >= half else -1)) % sects * cells + c))
    to_owner = [(b, a) for a, b in to_server]
    exchange = functools.partial(
        lax.all_to_all, axis_name="cell", split_axis=0, concat_axis=0, tiled=True
    )

    near_fields = lax.ppermute(atm_fields, axes, to_server)
    asking, slots = requests(ocn_map.T, lnd_map.T, cells)
    asked = exchange(asking)
    held = hold(atm_fields, near_fields)
    got = exchange(serve(asked, held, cells))
    ol, ll = ocn_local.T, lnd_local.T
    near, lt = near_mix(ol, ll, held, ocn_tiles, lnd_tiles)
    of, lf, send = far(
        slots, got, near, ocn_state, ice_state, ice_level.reshape(-1, BL), lnd_state,
        lnd_level.reshape(-1, BL), lt, ocn_tiles,
    )
    back = exchange(send)
    acc = near_back(ol, ll, of, lf, ocn_tiles, lnd_tiles)
    back, acc = lax.optimization_barrier((back, acc))
    away = lax.ppermute(collect(asked, back, None, True, cells), axes, to_owner)
    own = collect(asked, back, acc, False, cells)
    return own + away.astype(jnp.float32), of, lf


def solution(mesh):
    a = ("sect", "cell")
    in_specs = (
        P(None, a), P(None, a), P(None, a), P(a), P(None, a), P(a),
        P(a, None), P(a, None), P(a, None, None, None),
        P(a, None), P(a, None), P(a, None, None, None),
    )
    return jax.shard_map(
        functools.partial(per_device, mesh.shape["sect"], mesh.shape["cell"]),
        mesh=mesh,
        in_specs=in_specs,
        out_specs=(P(None, a), P(None, a), P(None, a)),
        check_vma=False,
    )
```

```python
import functools

import jax
import jax.numpy as jnp
from jax import lax
from jax.experimental import pallas as pl
from jax.experimental.pallas import tpu as pltpu
from jax.sharding import PartitionSpec as P

ocean_coef = (1.2, 0.9, 1.5, 0.7, 1.1, 1.3, 0.8, 1.0)
ice_coef = (0.5, 1.4, 0.6, 1.2, 0.9, 0.4, 1.6, 0.7)
land_coef = (0.8, 1.1, 0.6, 1.5, 0.7, 1.2, 1.0, 0.5)

BL = 128
AB_BITS = 5
AB = 1 << AB_BITS
KR = KL = 2
CAP = 15
GRANT, LARGE, SMALL = 60 << 20, 50 << 20, 8 << 20
CHAINS = 5
VMEM = pltpu.VMEM
SMEM = pltpu.SMEM
NN = (((1,), (0,)), ((), ()))
NT = (((1,), (1,)), ((), ()))


def dot(a, b, dims):
    return lax.dot_general(a, b, dims, preferred_element_type=jnp.float32)


def lanes(i):
    return pl.ds(pl.multiple_of(i * BL, BL), BL)


def whole(space=VMEM):
    return pl.BlockSpec(memory_space=space)


def column(values, width):
    row = lax.broadcasted_iota(jnp.int32, (8, BL), 0)
    out = jnp.full((8, BL), values[7], jnp.float32)
    for j in range(7):
        out = jnp.where(row == j, values[j], out)
    return jnp.concatenate([out] * (width // BL), axis=1)


def request_kernel(cells, om_ref, lm_ref, req_ref, slot_ref):
    sect = lax.axis_index("sect")
    cell_bits = cells.bit_length() - 1
    before = jnp.zeros((cells, 1), jnp.float32)
    req = jnp.zeros((cells, BL), jnp.float32)
    slot_ref[...] = jnp.zeros(slot_ref.shape, jnp.int32)
    row = 0
    for ref in (om_ref, lm_ref):
        n = ref.shape[1]
        earlier = lax.broadcasted_iota(jnp.int32, (n, n), 0) < lax.broadcasted_iota(
            jnp.int32, (n, n), 1
        )
        earlier = jnp.where(earlier, 1.0, 0.0).astype(jnp.bfloat16)
        for k in range(ref.shape[0]):
            src = ref[k : k + 1, :]
            owner = src >> AB_BITS
            col = owner & (cells - 1)
            value = (src & (AB - 1)) + jnp.where(owner >> cell_bits == sect, 0, AB)
            chosen = lax.broadcasted_iota(jnp.int32, (cells, n), 0) == col
            onehot = jnp.where(chosen, 1.0, 0.0)
            ranks = before + dot(onehot.astype(jnp.bfloat16), earlier, NN)
            rank = jnp.sum(jnp.where(chosen, ranks, 0.0), axis=0, keepdims=True)
            before = before + jnp.sum(onehot, axis=1, keepdims=True)
            place = lax.broadcasted_iota(jnp.int32, (BL, n), 0) == rank.astype(jnp.int32)
            place = jnp.where(place, 1.0, 0.0).astype(jnp.bfloat16)
            asked = jnp.where(chosen, (value + 1).astype(jnp.float32), 0.0)
            req = req + dot(asked.astype(jnp.bfloat16), place, NT)
            slot_ref[row : row + 1, :n] = col * CAP + rank.astype(jnp.int32)
            row += 1
    req_ref[...] = req.astype(jnp.int32) - 1


def requests(om, lm, cells):
    return pl.pallas_call(
        functools.partial(request_kernel, cells),
        out_shape=(
            jax.ShapeDtypeStruct((cells, BL), jnp.int32),
            jax.ShapeDtypeStruct((8, BL), jnp.int32),
        ),
        in_specs=[whole()] * 2,
        out_specs=[whole()] * 2,
        compiler_params=pltpu.CompilerParams(vmem_limit_bytes=GRANT),
        name="requests",
    )(om, lm)


def hold_kernel(own_ref, near_ref, out_ref):
    nf, width = own_ref.shape
    rows = lax.broadcasted_iota(jnp.int32, (nf, nf), 0)
    pick = 3 * (rows & 7) + (rows >> 3) == lax.broadcasted_iota(jnp.int32, (nf, nf), 1)
    pick = jnp.where(pick, 1.0, 0.0).astype(own_ref.dtype)
    for k, ref in enumerate((own_ref, near_ref)):
        for at in range(0, width, 8 * BL):
            part = dot(pick, ref[:, at : at + 8 * BL], NN)
            out_ref[:, k * width + at : k * width + at + 8 * BL] = part.astype(out_ref.dtype)


def hold(own, near):
    return pl.pallas_call(
        hold_kernel,
        out_shape=jax.ShapeDtypeStruct((own.shape[0], 2 * own.shape[1]), own.dtype),
        in_specs=[whole()] * 2,
        out_specs=whole(),
        compiler_params=pltpu.CompilerParams(vmem_limit_bytes=SMALL),
        cost_estimate=pl.CostEstimate(flops=1 << 20, bytes_accessed=4 << 20, transcendentals=0),
        name="hold",
    )(own, near)


def serve_kernel(cells, asked_ref, both, out_ref, made, out_sems):
    def out(c):
        part = pl.ds(c * CAP, CAP)
        return pltpu.make_async_copy(made.at[part], out_ref.at[part], out_sems.at[c])

    def body(c, _):
        for r in range(CAP):
            i = jnp.maximum(asked_ref[c, r], 0)
            made[c * CAP + r] = both[:, lanes(i)]
        out(c).start()
        return 0

    lax.fori_loop(0, cells, body, 0)
    for c in range(cells):
        out(c).wait()


def serve(asked, both, cells):
    shape = (cells * CAP, both.shape[0], BL)
    return pl.pallas_call(
        functools.partial(serve_kernel, cells),
        out_shape=jax.ShapeDtypeStruct(shape, both.dtype),
        in_specs=[whole(SMEM), whole()],
        out_specs=whole(pltpu.HBM),
        scratch_shapes=[VMEM(shape, both.dtype), pltpu.SemaphoreType.DMA((cells,))],
        compiler_params=pltpu.CompilerParams(vmem_limit_bytes=SMALL),
        name="serve",
    )(asked, both)


STEPS = 4
PARTS = (0, 4, 10, 16)


def tile_specs(ob, lb, half):
    return [
        pl.BlockSpec((ob // STEPS, 2, BL, BL), lambda i: (i, half, 0, 0)),
        pl.BlockSpec((lb // STEPS, 2, BL, BL), lambda i: (i, half, 0, 0)),
    ]


def near_mix_kernel(ol_ref, ll_ref, f_ref, ot_ref, lt_ref, out_ref):
    step = pl.program_id(0)
    at = 0
    for ids, tiles in ((ol_ref, ot_ref), (ll_ref, lt_ref)):
        n = tiles.shape[0]
        for b in range(n):
            src = [f_ref[:, lanes(ids[k, step * n + b])] for k in range(2)]
            out_ref[at] = dot(
                jnp.concatenate(src, axis=1), tiles[b].reshape(2 * BL, BL), NN
            )
            at += 1


def near_mix(ol, ll, fields, ot, lt):
    ob, lb = ot.shape[0], lt.shape[0]
    nf = fields.shape[0]
    return pl.pallas_call(
        near_mix_kernel,
        grid=(STEPS,),
        out_shape=jax.ShapeDtypeStruct((ob + lb, nf, BL), jnp.float32),
        in_specs=[
            whole(SMEM),
            whole(SMEM),
            pl.BlockSpec(fields.shape, lambda i: (0, 0)),
            *tile_specs(ob, lb, 1),
        ],
        out_specs=pl.BlockSpec(((ob + lb) // STEPS, nf, BL), lambda i: (i, 0, 0)),
        compiler_params=pltpu.CompilerParams(vmem_limit_bytes=52 << 20),
        cost_estimate=pl.CostEstimate(
            flops=2 * (ob + lb) * 2 * BL * BL * 128,
            bytes_accessed=(ob + lb) * 2 * BL * BL * 2,
            transcendentals=0,
        ),
        name="near_mix",
    )(ol, ll, fields, ot, lt)


def portions(ob, lb):
    cuts = [ob * p // 16 for p in PARTS]
    out = [[(0, lo, hi)] for lo, hi in zip(cuts[:-1], cuts[1:])]
    out[-1].append((1, 0, lb))
    return out


def far_kernel(
    slot_ref, got_ref, near, osv, isv, il, ls, ll, ot_hbm, lt_hbm, of_hbm, lf_hbm, send_hbm,
    ot, lt, of, lf, send, in_sems, out_sems,
):
    ob, lb = ot.shape[0], lt.shape[0]
    no, nl = ob // STEPS, lb // STEPS
    parts = portions(ob, lb)
    ins, outs = [], []
    for part in parts:
        for kind, lo, hi in part:
            hbm, on_chip = (lt_hbm, lt) if kind else (ot_hbm, ot)
            some = pl.ds(lo, hi - lo)
            copy = pltpu.make_async_copy(
                hbm.at[some, pl.ds(0, KR)], on_chip.at[some], in_sems.at[len(ins)]
            )
            copy.start()
            ins.append(copy)
            flux, flux_hbm = (lf, lf_hbm) if kind else (of, of_hbm)
            some = pl.ds(lo * BL, (hi - lo) * BL)
            outs.append(
                pltpu.make_async_copy(flux.at[:, some], flux_hbm.at[:, some], out_sems.at[len(outs)])
            )
    send[...] = jnp.zeros(send.shape, send.dtype)
    waits, sends = iter(ins), iter(outs)
    for part in parts:
        for _ in part:
            next(waits).wait()
        work = [(kind, b) for kind, lo, hi in part for b in range(lo, hi)]
        slots = [[slot_ref[2 * kind + k, b] for k in range(KR)] for kind, b in work]
        weights = [(lt if kind else ot)[b].reshape(KR * BL, BL) for kind, b in work]
        rows = []
        for (kind, b), pair, weight in zip(work, slots, weights):
            at = (b // nl) * (no + nl) + no + b % nl if kind else (b // no) * (no + nl) + b % no
            source = jnp.concatenate([got_ref[s] for s in pair], axis=1)
            rows.append(near[at] + dot(source, weight, NN))
        fluxes = []
        for kind, lo, hi in part:
            n = hi - lo
            mine = rows[len(fluxes) : len(fluxes) + n]
            u, v, t = (
                jnp.concatenate([row[8 * j : 8 * j + 8] for row in mine], axis=1) for j in range(3)
            )
            wind = jnp.sqrt(1.0 + u * u + v * v)
            here = slice(lo * BL, hi * BL)
            level = (ll if kind else il)[lo:hi, :].astype(jnp.float32) * 0.125
            level = [jnp.broadcast_to(level[j : j + 1], (8, BL)) for j in range(n)]
            frac = jnp.concatenate(level, axis=1)

            def bulk(factors, state):
                return column(factors, n * BL) * wind * (t - state[:, here])

            if kind:
                flux = frac * bulk(land_coef, ls)
                lf[:, here] = flux
            else:
                flux = (1.0 - frac) * bulk(ocean_coef, osv) + frac * bulk(ice_coef, isv)
                of[:, here] = flux
            next(sends).start()
            flux = flux.astype(jnp.bfloat16)
            fluxes += [flux[:, j * BL : (j + 1) * BL] for j in range(n)]
        for flux, pair, weight in zip(fluxes, slots, weights):
            terms = dot(flux, weight, NT).astype(send.dtype)
            for k in range(KR):
                send[pair[k]] = terms[:, k * BL : (k + 1) * BL]
    outs.append(pltpu.make_async_copy(send, send_hbm, out_sems.at[len(outs)]))
    outs[-1].start()
    for copy in outs:
        copy.wait()


def far(slots, got, near, os, ice, il, ls, ll, ot, lt):
    f32 = jnp.float32
    back = (got.shape[0], os.shape[0], BL)
    count = len(PARTS)
    return pl.pallas_call(
        far_kernel,
        out_shape=(
            jax.ShapeDtypeStruct(os.shape, f32),
            jax.ShapeDtypeStruct(ls.shape, f32),
            jax.ShapeDtypeStruct(back, jnp.bfloat16),
        ),
        in_specs=[whole(SMEM), *[whole()] * 7, *[whole(pl.ANY)] * 2],
        out_specs=[whole(pltpu.HBM)] * 3,
        scratch_shapes=[
            VMEM((ot.shape[0], KR, BL, BL), ot.dtype),
            VMEM((lt.shape[0], KR, BL, BL), lt.dtype),
            VMEM(os.shape, f32),
            VMEM(ls.shape, f32),
            VMEM(back, jnp.bfloat16),
            pltpu.SemaphoreType.DMA((count,)),
            pltpu.SemaphoreType.DMA((count + 1,)),
        ],
        compiler_params=pltpu.CompilerParams(vmem_limit_bytes=50 << 20),
        name="far",
    )(slots, got, near, os, ice, il, ls, ll, ot, lt)


def near_back_kernel(ol_ref, ll_ref, of_ref, lf_ref, ot_ref, lt_ref, out_ref):
    step = pl.program_id(0)

    @pl.when(step == 0)
    def _():
        out_ref[...] = jnp.zeros(out_ref.shape, out_ref.dtype)

    for ids, flux, tiles in ((ol_ref, of_ref, ot_ref), (ll_ref, lf_ref, lt_ref)):
        n = tiles.shape[0]
        for b in range(n):
            g = flux[:, b * BL : (b + 1) * BL].astype(jnp.bfloat16)
            terms = dot(g, tiles[b].reshape(2 * BL, BL), NT)
            for k in range(2):
                at = lanes(ids[k, step * n + b])
                out_ref[:, at] = out_ref[:, at] + terms[:, k * BL : (k + 1) * BL]


def near_back(ol, ll, of, lf, ot, lt):
    ob, lb = ot.shape[0], lt.shape[0]
    ns = of.shape[0]
    return pl.pallas_call(
        near_back_kernel,
        grid=(STEPS,),
        out_shape=jax.ShapeDtypeStruct((ns, AB * BL), jnp.float32),
        in_specs=[
            whole(SMEM),
            whole(SMEM),
            pl.BlockSpec((ns, ob // STEPS * BL), lambda i: (0, i)),
            pl.BlockSpec((ns, lb // STEPS * BL), lambda i: (0, i)),
            *tile_specs(ob, lb, 1),
        ],
        out_specs=pl.BlockSpec((ns, AB * BL), lambda i: (0, 0)),
        compiler_params=pltpu.CompilerParams(vmem_limit_bytes=GRANT),
        cost_estimate=pl.CostEstimate(
            flops=2 * (ob + lb) * 2 * BL * BL * 128,
            bytes_accessed=(ob + lb) * 2 * BL * BL * 2,
            transcendentals=0,
        ),
        name="near_back",
    )(ol, ll, of, lf, ot, lt)


def collect_kernel(cells, neighbours, asked_ref, back_ref, *refs):
    if neighbours:
        out_ref, *totals = refs
    else:
        acc_ref, out_ref, acc, sem, *totals = refs
        load = pltpu.make_async_copy(acc_ref, acc, sem)
        load.start()
        totals = [acc, *totals]
    cell = lax.axis_index("cell")
    half = cells // 2
    for total in totals[-CHAINS:]:
        total[...] = jnp.zeros(total.shape, jnp.float32)

    def body(c, _):
        far_one = jnp.logical_or(c <= cell - half, c > cell + half)

        @pl.when(far_one == neighbours)
        def _():
            for r in range(CAP):
                total = totals[r % CHAINS - CHAINS]
                i = asked_ref[c, r]
                at = lanes(jnp.where(i < 0, AB, i & (AB - 1)))
                total[:, at] = total[:, at] + back_ref[c * CAP + r].astype(jnp.float32)

        return 0

    lax.fori_loop(0, cells, body, 0)
    if not neighbours:
        load.wait()
    for b in range(AB):
        here = slice(b * BL, (b + 1) * BL)
        total = functools.reduce(jnp.add, [ref[:, here] for ref in totals])
        out_ref[:, here] = total.astype(out_ref.dtype)


def collect(asked, back, acc, neighbours, cells):
    ns = back.shape[1]
    shape = (ns, AB * BL)
    accs, more = (), []
    if acc is not None:
        accs, more = (acc,), [VMEM(shape, jnp.float32), pltpu.SemaphoreType.DMA(())]
    return pl.pallas_call(
        functools.partial(collect_kernel, cells, neighbours),
        out_shape=jax.ShapeDtypeStruct(shape, jnp.float32 if accs else back.dtype),
        in_specs=[whole(SMEM), whole(), *[whole(pltpu.HBM)] * len(accs)],
        out_specs=whole(),
        scratch_shapes=[*more, *[VMEM((ns, (AB + 1) * BL), jnp.float32)] * CHAINS],
        compiler_params=pltpu.CompilerParams(vmem_limit_bytes=SMALL),
        cost_estimate=pl.CostEstimate(
            flops=1 << 20, bytes_accessed=4 << 20, transcendentals=0
        ),
        name="collect_far" if neighbours else "collect_own",
    )(asked, back, *accs)


def per_device(
    sects, cells, atm_fields, ocn_state, ice_state, ice_level, lnd_state, lnd_level,
    ocn_map, ocn_local, ocn_tiles, lnd_map, lnd_local, lnd_tiles,
):
    axes = ("sect", "cell")
    count = sects * cells
    half = cells // 2
    to_server = []
    for q in range(count):
        s, c = divmod(q, cells)
        to_server.append((q, (s + (1 if c >= half else -1)) % sects * cells + c))
    to_owner = [(b, a) for a, b in to_server]
    exchange = functools.partial(
        lax.all_to_all, axis_name="cell", split_axis=0, concat_axis=0, tiled=True
    )

    near_fields = lax.ppermute(atm_fields, axes, to_server)
    asking, slots = requests(ocn_map.T, lnd_map.T, cells)
    asked = exchange(asking)
    held = hold(atm_fields, near_fields)
    got = exchange(serve(asked, held, cells))
    ol, ll = ocn_local.T, lnd_local.T
    near = near_mix(ol, ll, held, ocn_tiles, lnd_tiles)
    of, lf, send = far(
        slots, got, near, ocn_state, ice_state, ice_level.reshape(-1, BL), lnd_state,
        lnd_level.reshape(-1, BL), ocn_tiles, lnd_tiles,
    )
    back = exchange(send)
    acc = near_back(ol, ll, of, lf, ocn_tiles, lnd_tiles)
    back, acc = lax.optimization_barrier((back, acc))
    away = lax.ppermute(collect(asked, back, None, True, cells), axes, to_owner)
    own = collect(asked, back, acc, False, cells)
    return own + away.astype(jnp.float32), of, lf


def solution(mesh):
    a = ("sect", "cell")
    in_specs = (
        P(None, a), P(None, a), P(None, a), P(a), P(None, a), P(a),
        P(a, None), P(a, None), P(a, None, None, None),
        P(a, None), P(a, None), P(a, None, None, None),
    )
    return jax.shard_map(
        functools.partial(per_device, mesh.shape["sect"], mesh.shape["cell"]),
        mesh=mesh,
        in_specs=in_specs,
        out_specs=(P(None, a), P(None, a), P(None, a)),
        check_vma=False,
    )
```

```python
import functools

import jax
import jax.numpy as jnp
from jax import lax
from jax.experimental import pallas as pl
from jax.experimental.pallas import tpu as pltpu
from jax.sharding import PartitionSpec as P

ocean_coef = (1.2, 0.9, 1.5, 0.7, 1.1, 1.3, 0.8, 1.0)
ice_coef = (0.5, 1.4, 0.6, 1.2, 0.9, 0.4, 1.6, 0.7)
land_coef = (0.8, 1.1, 0.6, 1.5, 0.7, 1.2, 1.0, 0.5)

BL = 128
AB_BITS = 5
AB = 1 << AB_BITS
KR = KL = 2
CAP = 15
GRANT, LARGE, SMALL = 60 << 20, 50 << 20, 8 << 20
CHAINS = 5
VMEM = pltpu.VMEM
SMEM = pltpu.SMEM
NN = (((1,), (0,)), ((), ()))
NT = (((1,), (1,)), ((), ()))


def dot(a, b, dims):
    return lax.dot_general(a, b, dims, preferred_element_type=jnp.float32)


def lanes(i):
    return pl.ds(pl.multiple_of(i * BL, BL), BL)


def whole(space=VMEM):
    return pl.BlockSpec(memory_space=space)


def column(values, width):
    row = lax.broadcasted_iota(jnp.int32, (8, BL), 0)
    out = jnp.full((8, BL), values[7], jnp.float32)
    for j in range(7):
        out = jnp.where(row == j, values[j], out)
    return jnp.concatenate([out] * (width // BL), axis=1)


def request_kernel(cells, om_ref, lm_ref, req_ref, slot_ref):
    sect = lax.axis_index("sect")
    cell_bits = cells.bit_length() - 1
    before = jnp.zeros((cells, 1), jnp.float32)
    req = jnp.zeros((cells, BL), jnp.float32)
    slot_ref[...] = jnp.zeros(slot_ref.shape, jnp.int32)
    row = 0
    for ref in (om_ref, lm_ref):
        n = ref.shape[1]
        earlier = lax.broadcasted_iota(jnp.int32, (n, n), 0) < lax.broadcasted_iota(
            jnp.int32, (n, n), 1
        )
        earlier = jnp.where(earlier, 1.0, 0.0).astype(jnp.bfloat16)
        for k in range(ref.shape[0]):
            src = ref[k : k + 1, :]
            owner = src >> AB_BITS
            col = owner & (cells - 1)
            value = (src & (AB - 1)) + jnp.where(owner >> cell_bits == sect, 0, AB)
            chosen = lax.broadcasted_iota(jnp.int32, (cells, n), 0) == col
            onehot = jnp.where(chosen, 1.0, 0.0)
            ranks = before + dot(onehot.astype(jnp.bfloat16), earlier, NN)
            rank = jnp.sum(jnp.where(chosen, ranks, 0.0), axis=0, keepdims=True)
            before = before + jnp.sum(onehot, axis=1, keepdims=True)
            place = lax.broadcasted_iota(jnp.int32, (BL, n), 0) == rank.astype(jnp.int32)
            place = jnp.where(place, 1.0, 0.0).astype(jnp.bfloat16)
            asked = jnp.where(chosen, (value + 1).astype(jnp.float32), 0.0)
            req = req + dot(asked.astype(jnp.bfloat16), place, NT)
            slot_ref[row : row + 1, :n] = col * CAP + rank.astype(jnp.int32)
            row += 1
    req_ref[...] = req.astype(jnp.int32) - 1


def requests(om, lm, cells):
    return pl.pallas_call(
        functools.partial(request_kernel, cells),
        out_shape=(
            jax.ShapeDtypeStruct((cells, BL), jnp.int32),
            jax.ShapeDtypeStruct((8, BL), jnp.int32),
        ),
        in_specs=[whole()] * 2,
        out_specs=[whole()] * 2,
        compiler_params=pltpu.CompilerParams(vmem_limit_bytes=GRANT),
        name="requests",
    )(om, lm)


def hold_kernel(own_ref, near_ref, out_ref):
    nf, width = own_ref.shape
    rows = lax.broadcasted_iota(jnp.int32, (nf, nf), 0)
    pick = 3 * (rows & 7) + (rows >> 3) == lax.broadcasted_iota(jnp.int32, (nf, nf), 1)
    pick = jnp.where(pick, 1.0, 0.0).astype(own_ref.dtype)
    for k, ref in enumerate((own_ref, near_ref)):
        for at in range(0, width, 8 * BL):
            part = dot(pick, ref[:, at : at + 8 * BL], NN)
            out_ref[:, k * width + at : k * width + at + 8 * BL] = part.astype(out_ref.dtype)


def hold(own, near):
    return pl.pallas_call(
        hold_kernel,
        out_shape=jax.ShapeDtypeStruct((own.shape[0], 2 * own.shape[1]), own.dtype),
        in_specs=[whole()] * 2,
        out_specs=whole(),
        compiler_params=pltpu.CompilerParams(vmem_limit_bytes=SMALL),
        cost_estimate=pl.CostEstimate(flops=1 << 20, bytes_accessed=4 << 20, transcendentals=0),
        name="hold",
    )(own, near)


def serve_kernel(cells, asked_ref, both, out_ref, made, out_sems):
    def out(c):
        part = pl.ds(c * CAP, CAP)
        return pltpu.make_async_copy(made.at[part], out_ref.at[part], out_sems.at[c])

    def body(c, _):
        for r in range(CAP):
            i = jnp.maximum(asked_ref[c, r], 0)
            made[c * CAP + r] = both[:, lanes(i)]
        out(c).start()
        return 0

    lax.fori_loop(0, cells, body, 0)
    for c in range(cells):
        out(c).wait()


def serve(asked, both, cells):
    shape = (cells * CAP, both.shape[0], BL)
    return pl.pallas_call(
        functools.partial(serve_kernel, cells),
        out_shape=jax.ShapeDtypeStruct(shape, both.dtype),
        in_specs=[whole(SMEM), whole()],
        out_specs=whole(pltpu.HBM),
        scratch_shapes=[VMEM(shape, both.dtype), pltpu.SemaphoreType.DMA((cells,))],
        compiler_params=pltpu.CompilerParams(vmem_limit_bytes=SMALL),
        name="serve",
    )(asked, both)


STEPS = 4
PARTS = (0, 4, 10, 16)


def tile_specs(ob, lb, half):
    return [
        pl.BlockSpec((ob // STEPS, 2, BL, BL), lambda i: (i, half, 0, 0)),
        pl.BlockSpec((lb // STEPS, 2, BL, BL), lambda i: (i, half, 0, 0)),
    ]


def near_mix_kernel(ol_ref, ll_ref, f_ref, ot_ref, lt_ref, out_ref):
    step = pl.program_id(0)
    at = 0
    for ids, tiles in ((ol_ref, ot_ref), (ll_ref, lt_ref)):
        n = tiles.shape[0]
        for b in range(n):
            src = [f_ref[:, lanes(ids[k, step * n + b])] for k in range(2)]
            out_ref[at] = dot(
                jnp.concatenate(src, axis=1), tiles[b].reshape(2 * BL, BL), NN
            )
            at += 1


def near_mix(ol, ll, fields, ot, lt):
    ob, lb = ot.shape[0], lt.shape[0]
    nf = fields.shape[0]
    return pl.pallas_call(
        near_mix_kernel,
        grid=(STEPS,),
        out_shape=jax.ShapeDtypeStruct((ob + lb, nf, BL), jnp.float32),
        in_specs=[
            whole(SMEM),
            whole(SMEM),
            pl.BlockSpec(fields.shape, lambda i: (0, 0)),
            *tile_specs(ob, lb, 1),
        ],
        out_specs=pl.BlockSpec(((ob + lb) // STEPS, nf, BL), lambda i: (i, 0, 0)),
        compiler_params=pltpu.CompilerParams(vmem_limit_bytes=52 << 20),
        cost_estimate=pl.CostEstimate(
            flops=2 * (ob + lb) * 2 * BL * BL * 128,
            bytes_accessed=(ob + lb) * 2 * BL * BL * 2,
            transcendentals=0,
        ),
        name="near_mix",
    )(ol, ll, fields, ot, lt)


def portions(ob, lb):
    cuts = [ob * p // 16 for p in PARTS]
    out = [[(0, lo, hi)] for lo, hi in zip(cuts[:-1], cuts[1:])]
    out[-1].append((1, 0, lb))
    return out


def far_kernel(
    slot_hbm, got_ref, near, osv, isv, il, ls, ll, ot_hbm, lt_hbm, of_hbm, lf_hbm, send_hbm,
    slot_ref, ot, lt, of, lf, send, in_sems, out_sems, slot_sem,
):
    ob, lb = ot.shape[0], lt.shape[0]
    no, nl = ob // STEPS, lb // STEPS
    parts = portions(ob, lb)
    ins, outs = [], []
    for part in parts:
        for kind, lo, hi in part:
            hbm, on_chip = (lt_hbm, lt) if kind else (ot_hbm, ot)
            some = pl.ds(lo, hi - lo)
            copy = pltpu.make_async_copy(
                hbm.at[some, pl.ds(0, KR)], on_chip.at[some], in_sems.at[len(ins)]
            )
            copy.start()
            ins.append(copy)
            flux, flux_hbm = (lf, lf_hbm) if kind else (of, of_hbm)
            some = pl.ds(lo * BL, (hi - lo) * BL)
            outs.append(
                pltpu.make_async_copy(flux.at[:, some], flux_hbm.at[:, some], out_sems.at[len(outs)])
            )
        if part is parts[0]:
            load = pltpu.make_async_copy(slot_hbm, slot_ref, slot_sem)
            load.start()
    send[...] = jnp.zeros(send.shape, send.dtype)
    load.wait()
    waits, sends = iter(ins), iter(outs)
    for part in parts:
        for _ in part:
            next(waits).wait()
        work = [(kind, b) for kind, lo, hi in part for b in range(lo, hi)]
        slots = [[slot_ref[2 * kind + k, b] for k in range(KR)] for kind, b in work]
        weights = [(lt if kind else ot)[b].reshape(KR * BL, BL) for kind, b in work]
        rows = []
        for (kind, b), pair, weight in zip(work, slots, weights):
            at = (b // nl) * (no + nl) + no + b % nl if kind else (b // no) * (no + nl) + b % no
            source = jnp.concatenate([got_ref[s] for s in pair], axis=1)
            rows.append(near[at] + dot(source, weight, NN))
        fluxes = []
        for kind, lo, hi in part:
            n = hi - lo
            mine = rows[len(fluxes) : len(fluxes) + n]
            u, v, t = (
                jnp.concatenate([row[8 * j : 8 * j + 8] for row in mine], axis=1) for j in range(3)
            )
            wind = jnp.sqrt(1.0 + u * u + v * v)
            here = slice(lo * BL, hi * BL)
            level = (ll if kind else il)[lo:hi, :].astype(jnp.float32) * 0.125
            level = [jnp.broadcast_to(level[j : j + 1], (8, BL)) for j in range(n)]
            frac = jnp.concatenate(level, axis=1)

            def bulk(factors, state):
                return column(factors, n * BL) * wind * (t - state[:, here])

            if kind:
                flux = frac * bulk(land_coef, ls)
                lf[:, here] = flux
            else:
                flux = (1.0 - frac) * bulk(ocean_coef, osv) + frac * bulk(ice_coef, isv)
                of[:, here] = flux
            next(sends).start()
            flux = flux.astype(jnp.bfloat16)
            fluxes += [flux[:, j * BL : (j + 1) * BL] for j in range(n)]
        for flux, pair, weight in zip(fluxes, slots, weights):
            terms = dot(flux, weight, NT).astype(send.dtype)
            for k in range(KR):
                send[pair[k]] = terms[:, k * BL : (k + 1) * BL]
    outs.append(pltpu.make_async_copy(send, send_hbm, out_sems.at[len(outs)]))
    outs[-1].start()
    for copy in outs:
        copy.wait()


def far(slots, got, near, os, ice, il, ls, ll, ot, lt):
    f32 = jnp.float32
    back = (got.shape[0], os.shape[0], BL)
    count = len(PARTS)
    return pl.pallas_call(
        far_kernel,
        out_shape=(
            jax.ShapeDtypeStruct(os.shape, f32),
            jax.ShapeDtypeStruct(ls.shape, f32),
            jax.ShapeDtypeStruct(back, jnp.bfloat16),
        ),
        in_specs=[whole(pl.ANY), *[whole()] * 7, *[whole(pl.ANY)] * 2],
        out_specs=[whole(pltpu.HBM)] * 3,
        scratch_shapes=[
            SMEM(slots.shape, slots.dtype),
            VMEM((ot.shape[0], KR, BL, BL), ot.dtype),
            VMEM((lt.shape[0], KR, BL, BL), lt.dtype),
            VMEM(os.shape, f32),
            VMEM(ls.shape, f32),
            VMEM(back, jnp.bfloat16),
            pltpu.SemaphoreType.DMA((count,)),
            pltpu.SemaphoreType.DMA((count + 1,)),
            pltpu.SemaphoreType.DMA(()),
        ],
        compiler_params=pltpu.CompilerParams(vmem_limit_bytes=50 << 20),
        name="far",
    )(slots, got, near, os, ice, il, ls, ll, ot, lt)


def near_back_kernel(ol_ref, ll_ref, of_ref, lf_ref, ot_ref, lt_ref, out_ref):
    step = pl.program_id(0)

    @pl.when(step == 0)
    def _():
        out_ref[...] = jnp.zeros(out_ref.shape, out_ref.dtype)

    for ids, flux, tiles in ((ol_ref, of_ref, ot_ref), (ll_ref, lf_ref, lt_ref)):
        n = tiles.shape[0]
        for b in range(n):
            g = flux[:, b * BL : (b + 1) * BL].astype(jnp.bfloat16)
            terms = dot(g, tiles[b].reshape(2 * BL, BL), NT)
            for k in range(2):
                at = lanes(ids[k, step * n + b])
                out_ref[:, at] = out_ref[:, at] + terms[:, k * BL : (k + 1) * BL]


def near_back(ol, ll, of, lf, ot, lt):
    ob, lb = ot.shape[0], lt.shape[0]
    ns = of.shape[0]
    return pl.pallas_call(
        near_back_kernel,
        grid=(STEPS,),
        out_shape=jax.ShapeDtypeStruct((ns, AB * BL), jnp.float32),
        in_specs=[
            whole(SMEM),
            whole(SMEM),
            pl.BlockSpec((ns, ob // STEPS * BL), lambda i: (0, i)),
            pl.BlockSpec((ns, lb // STEPS * BL), lambda i: (0, i)),
            *tile_specs(ob, lb, 1),
        ],
        out_specs=pl.BlockSpec((ns, AB * BL), lambda i: (0, 0)),
        compiler_params=pltpu.CompilerParams(vmem_limit_bytes=GRANT),
        cost_estimate=pl.CostEstimate(
            flops=2 * (ob + lb) * 2 * BL * BL * 128,
            bytes_accessed=(ob + lb) * 2 * BL * BL * 2,
            transcendentals=0,
        ),
        name="near_back",
    )(ol, ll, of, lf, ot, lt)


def collect_kernel(cells, neighbours, asked_hbm, back_ref, *refs):
    asked_ref, asked_sem, *refs = refs[-2:] + refs[:-2]
    ask = pltpu.make_async_copy(asked_hbm, asked_ref, asked_sem)
    ask.start()
    if neighbours:
        out_ref, *totals = refs
    else:
        acc_ref, out_ref, acc, sem, *totals = refs
        load = pltpu.make_async_copy(acc_ref, acc, sem)
        load.start()
        totals = [acc, *totals]
    cell = lax.axis_index("cell")
    half = cells // 2
    for total in totals[-CHAINS:]:
        total[...] = jnp.zeros(total.shape, jnp.float32)
    ask.wait()

    def body(c, _):
        far_one = jnp.logical_or(c <= cell - half, c > cell + half)

        @pl.when(far_one == neighbours)
        def _():
            for r in range(CAP):
                total = totals[r % CHAINS - CHAINS]
                i = asked_ref[c, r]
                at = lanes(jnp.where(i < 0, AB, i & (AB - 1)))
                total[:, at] = total[:, at] + back_ref[c * CAP + r].astype(jnp.float32)

        return 0

    lax.fori_loop(0, cells, body, 0)
    if not neighbours:
        load.wait()
    for b in range(AB):
        here = slice(b * BL, (b + 1) * BL)
        total = functools.reduce(jnp.add, [ref[:, here] for ref in totals])
        out_ref[:, here] = total.astype(out_ref.dtype)


def collect(asked, back, acc, neighbours, cells):
    ns = back.shape[1]
    shape = (ns, AB * BL)
    accs, more = (), []
    if acc is not None:
        accs, more = (acc,), [VMEM(shape, jnp.float32), pltpu.SemaphoreType.DMA(())]
    return pl.pallas_call(
        functools.partial(collect_kernel, cells, neighbours),
        out_shape=jax.ShapeDtypeStruct(shape, jnp.float32 if accs else back.dtype),
        in_specs=[whole(pl.ANY), whole(), *[whole(pltpu.HBM)] * len(accs)],
        out_specs=whole(),
        scratch_shapes=[
            *more,
            *[VMEM((ns, (AB + 1) * BL), jnp.float32)] * CHAINS,
            SMEM(asked.shape, asked.dtype),
            pltpu.SemaphoreType.DMA(()),
        ],
        compiler_params=pltpu.CompilerParams(vmem_limit_bytes=SMALL),
        cost_estimate=pl.CostEstimate(
            flops=1 << 20, bytes_accessed=4 << 20, transcendentals=0
        ),
        name="collect_far" if neighbours else "collect_own",
    )(asked, back, *accs)


def per_device(
    sects, cells, atm_fields, ocn_state, ice_state, ice_level, lnd_state, lnd_level,
    ocn_map, ocn_local, ocn_tiles, lnd_map, lnd_local, lnd_tiles,
):
    axes = ("sect", "cell")
    count = sects * cells
    half = cells // 2
    to_server = []
    for q in range(count):
        s, c = divmod(q, cells)
        to_server.append((q, (s + (1 if c >= half else -1)) % sects * cells + c))
    to_owner = [(b, a) for a, b in to_server]
    exchange = functools.partial(
        lax.all_to_all, axis_name="cell", split_axis=0, concat_axis=0, tiled=True
    )

    near_fields = lax.ppermute(atm_fields, axes, to_server)
    asking, slots = requests(ocn_map.T, lnd_map.T, cells)
    asked = exchange(asking)
    held = hold(atm_fields, near_fields)
    got = exchange(serve(asked, held, cells))
    ol, ll = ocn_local.T, lnd_local.T
    near = near_mix(ol, ll, held, ocn_tiles, lnd_tiles)
    of, lf, send = far(
        slots, got, near, ocn_state, ice_state, ice_level.reshape(-1, BL), lnd_state,
        lnd_level.reshape(-1, BL), ocn_tiles, lnd_tiles,
    )
    back = exchange(send)
    acc = near_back(ol, ll, of, lf, ocn_tiles, lnd_tiles)
    back, acc = lax.optimization_barrier((back, acc))
    away = lax.ppermute(collect(asked, back, None, True, cells), axes, to_owner)
    own = collect(asked, back, acc, False, cells)
    return own + away.astype(jnp.float32), of, lf


def solution(mesh):
    a = ("sect", "cell")
    in_specs = (
        P(None, a), P(None, a), P(None, a), P(a), P(None, a), P(a),
        P(a, None), P(a, None), P(a, None, None, None),
        P(a, None), P(a, None), P(a, None, None, None),
    )
    return jax.shard_map(
        functools.partial(per_device, mesh.shape["sect"], mesh.shape["cell"]),
        mesh=mesh,
        in_specs=in_specs,
        out_specs=(P(None, a), P(None, a), P(None, a)),
        check_vma=False,
    )
```

```python
import functools

import jax
import jax.numpy as jnp
from jax import lax
from jax.experimental import pallas as pl
from jax.experimental.pallas import tpu as pltpu
from jax.sharding import PartitionSpec as P

ocean_coef = (1.2, 0.9, 1.5, 0.7, 1.1, 1.3, 0.8, 1.0)
ice_coef = (0.5, 1.4, 0.6, 1.2, 0.9, 0.4, 1.6, 0.7)
land_coef = (0.8, 1.1, 0.6, 1.5, 0.7, 1.2, 1.0, 0.5)

BL = 128
AB_BITS = 5
AB = 1 << AB_BITS
KR = KL = 2
CAP = 15
GRANT, LARGE, SMALL = 60 << 20, 50 << 20, 8 << 20
CHAINS = 5
VMEM = pltpu.VMEM
SMEM = pltpu.SMEM
NN = (((1,), (0,)), ((), ()))
NT = (((1,), (1,)), ((), ()))


def dot(a, b, dims):
    return lax.dot_general(a, b, dims, preferred_element_type=jnp.float32)


def lanes(i):
    return pl.ds(pl.multiple_of(i * BL, BL), BL)


def lanes_from(first):
    return pl.ds(pl.multiple_of(first, BL), BL)


def whole(space=VMEM):
    return pl.BlockSpec(memory_space=space)


def column(values, width):
    row = lax.broadcasted_iota(jnp.int32, (8, BL), 0)
    out = jnp.full((8, BL), values[7], jnp.float32)
    for j in range(7):
        out = jnp.where(row == j, values[j], out)
    return jnp.concatenate([out] * (width // BL), axis=1)


def request_kernel(cells, om_ref, lm_ref, req_ref, slot_ref):
    sect = lax.axis_index("sect")
    cell_bits = cells.bit_length() - 1
    before = jnp.zeros((cells, 1), jnp.float32)
    req = jnp.zeros((cells, BL), jnp.float32)
    slot_ref[...] = jnp.zeros(slot_ref.shape, jnp.int32)
    row = 0
    for ref in (om_ref, lm_ref):
        n = ref.shape[1]
        earlier = lax.broadcasted_iota(jnp.int32, (n, n), 0) < lax.broadcasted_iota(
            jnp.int32, (n, n), 1
        )
        earlier = jnp.where(earlier, 1.0, 0.0).astype(jnp.bfloat16)
        for k in range(ref.shape[0]):
            src = ref[k : k + 1, :]
            owner = src >> AB_BITS
            col = owner & (cells - 1)
            value = (src & (AB - 1)) + jnp.where(owner >> cell_bits == sect, 0, AB)
            chosen = lax.broadcasted_iota(jnp.int32, (cells, n), 0) == col
            onehot = jnp.where(chosen, 1.0, 0.0)
            ranks = before + dot(onehot.astype(jnp.bfloat16), earlier, NN)
            rank = jnp.sum(jnp.where(chosen, ranks, 0.0), axis=0, keepdims=True)
            before = before + jnp.sum(onehot, axis=1, keepdims=True)
            place = lax.broadcasted_iota(jnp.int32, (BL, n), 0) == rank.astype(jnp.int32)
            place = jnp.where(place, 1.0, 0.0).astype(jnp.bfloat16)
            asked = jnp.where(chosen, (value + 1).astype(jnp.float32), 0.0)
            req = req + dot(asked.astype(jnp.bfloat16), place, NT)
            slot_ref[row : row + 1, :n] = col * CAP + rank.astype(jnp.int32)
            row += 1
    asked = req.astype(jnp.int32)
    req_ref[...] = jnp.where(asked == 0, 2 * AB, asked - 1) * BL


def requests(om, lm, cells):
    return pl.pallas_call(
        functools.partial(request_kernel, cells),
        out_shape=(
            jax.ShapeDtypeStruct((cells, BL), jnp.int32),
            jax.ShapeDtypeStruct((8, BL), jnp.int32),
        ),
        in_specs=[whole()] * 2,
        out_specs=[whole()] * 2,
        compiler_params=pltpu.CompilerParams(vmem_limit_bytes=GRANT),
        name="requests",
    )(om, lm)


def hold_kernel(own_ref, near_ref, out_ref):
    nf, width = own_ref.shape
    rows = lax.broadcasted_iota(jnp.int32, (nf, nf), 0)
    pick = 3 * (rows & 7) + (rows >> 3) == lax.broadcasted_iota(jnp.int32, (nf, nf), 1)
    pick = jnp.where(pick, 1.0, 0.0).astype(own_ref.dtype)
    for k, ref in enumerate((own_ref, near_ref)):
        for at in range(0, width, 8 * BL):
            part = dot(pick, ref[:, at : at + 8 * BL], NN)
            out_ref[:, k * width + at : k * width + at + 8 * BL] = part.astype(out_ref.dtype)
    out_ref[:, 2 * width :] = jnp.zeros((nf, BL), out_ref.dtype)


def hold(own, near):
    return pl.pallas_call(
        hold_kernel,
        out_shape=jax.ShapeDtypeStruct((own.shape[0], 2 * own.shape[1] + BL), own.dtype),
        in_specs=[whole()] * 2,
        out_specs=whole(),
        compiler_params=pltpu.CompilerParams(vmem_limit_bytes=SMALL),
        cost_estimate=pl.CostEstimate(flops=1 << 20, bytes_accessed=4 << 20, transcendentals=0),
        name="hold",
    )(own, near)


def serve_kernel(cells, asked_ref, both, out_ref, made, out_sems):
    def out(c):
        part = pl.ds(c * CAP, CAP)
        return pltpu.make_async_copy(made.at[part], out_ref.at[part], out_sems.at[c])

    def body(c, _):
        for r in range(CAP):
            made[c * CAP + r] = both[:, lanes_from(asked_ref[c, r])]
        out(c).start()
        return 0

    lax.fori_loop(0, cells, body, 0)
    for c in range(cells):
        out(c).wait()


def serve(asked, both, cells):
    shape = (cells * CAP, both.shape[0], BL)
    return pl.pallas_call(
        functools.partial(serve_kernel, cells),
        out_shape=jax.ShapeDtypeStruct(shape, both.dtype),
        in_specs=[whole(SMEM), whole()],
        out_specs=whole(pltpu.HBM),
        scratch_shapes=[VMEM(shape, both.dtype), pltpu.SemaphoreType.DMA((cells,))],
        compiler_params=pltpu.CompilerParams(vmem_limit_bytes=SMALL),
        name="serve",
    )(asked, both)


STEPS = 4
PARTS = (0, 4, 10, 16)


def tile_specs(ob, lb, half):
    return [
        pl.BlockSpec((ob // STEPS, 2, BL, BL), lambda i: (i, half, 0, 0)),
        pl.BlockSpec((lb // STEPS, 2, BL, BL), lambda i: (i, half, 0, 0)),
    ]


def near_mix_kernel(ol_ref, ll_ref, f_ref, ot_ref, lt_ref, out_ref):
    step = pl.program_id(0)
    at = 0
    for ids, tiles in ((ol_ref, ot_ref), (ll_ref, lt_ref)):
        n = tiles.shape[0]
        for b in range(n):
            src = [f_ref[:, lanes(ids[k, step * n + b])] for k in range(2)]
            out_ref[at] = dot(
                jnp.concatenate(src, axis=1), tiles[b].reshape(2 * BL, BL), NN
            )
            at += 1


def near_mix(ol, ll, fields, ot, lt):
    ob, lb = ot.shape[0], lt.shape[0]
    nf = fields.shape[0]
    return pl.pallas_call(
        near_mix_kernel,
        grid=(STEPS,),
        out_shape=jax.ShapeDtypeStruct((ob + lb, nf, BL), jnp.float32),
        in_specs=[
            whole(SMEM),
            whole(SMEM),
            pl.BlockSpec(fields.shape, lambda i: (0, 0)),
            *tile_specs(ob, lb, 1),
        ],
        out_specs=pl.BlockSpec(((ob + lb) // STEPS, nf, BL), lambda i: (i, 0, 0)),
        compiler_params=pltpu.CompilerParams(vmem_limit_bytes=52 << 20),
        cost_estimate=pl.CostEstimate(
            flops=2 * (ob + lb) * 2 * BL * BL * 128,
            bytes_accessed=(ob + lb) * 2 * BL * BL * 2,
            transcendentals=0,
        ),
        name="near_mix",
    )(ol, ll, fields, ot, lt)


def portions(ob, lb):
    cuts = [ob * p // 16 for p in PARTS]
    out = [[(0, lo, hi)] for lo, hi in zip(cuts[:-1], cuts[1:])]
    out[-1].append((1, 0, lb))
    return out


def far_kernel(
    slot_hbm, got_ref, near, osv, isv, il, ls, ll, ot_hbm, lt_hbm, of_hbm, lf_hbm, send_hbm,
    slot_ref, ot, lt, of, lf, send, in_sems, out_sems, slot_sem,
):
    ob, lb = ot.shape[0], lt.shape[0]
    no, nl = ob // STEPS, lb // STEPS
    parts = portions(ob, lb)
    ins, outs = [], []
    for part in parts:
        for kind, lo, hi in part:
            hbm, on_chip = (lt_hbm, lt) if kind else (ot_hbm, ot)
            some = pl.ds(lo, hi - lo)
            copy = pltpu.make_async_copy(
                hbm.at[some, pl.ds(0, KR)], on_chip.at[some], in_sems.at[len(ins)]
            )
            copy.start()
            ins.append(copy)
            flux, flux_hbm = (lf, lf_hbm) if kind else (of, of_hbm)
            some = pl.ds(lo * BL, (hi - lo) * BL)
            outs.append(
                pltpu.make_async_copy(flux.at[:, some], flux_hbm.at[:, some], out_sems.at[len(outs)])
            )
        if part is parts[0]:
            load = pltpu.make_async_copy(slot_hbm, slot_ref, slot_sem)
            load.start()
    send[...] = jnp.zeros(send.shape, send.dtype)
    load.wait()
    waits, sends = iter(ins), iter(outs)
    for part in parts:
        for _ in part:
            next(waits).wait()
        work = [(kind, b) for kind, lo, hi in part for b in range(lo, hi)]
        slots = [[slot_ref[2 * kind + k, b] for k in range(KR)] for kind, b in work]
        weights = [(lt if kind else ot)[b].reshape(KR * BL, BL) for kind, b in work]
        rows = []
        for (kind, b), pair, weight in zip(work, slots, weights):
            at = (b // nl) * (no + nl) + no + b % nl if kind else (b // no) * (no + nl) + b % no
            source = jnp.concatenate([got_ref[s] for s in pair], axis=1)
            rows.append(near[at] + dot(source, weight, NN))
        fluxes = []
        for kind, lo, hi in part:
            n = hi - lo
            mine = rows[len(fluxes) : len(fluxes) + n]
            u, v, t = (
                jnp.concatenate([row[8 * j : 8 * j + 8] for row in mine], axis=1) for j in range(3)
            )
            wind = jnp.sqrt(1.0 + u * u + v * v)
            here = slice(lo * BL, hi * BL)
            level = (ll if kind else il)[lo:hi, :].astype(jnp.float32) * 0.125
            level = [jnp.broadcast_to(level[j : j + 1], (8, BL)) for j in range(n)]
            frac = jnp.concatenate(level, axis=1)

            def bulk(factors, state):
                return column(factors, n * BL) * wind * (t - state[:, here])

            if kind:
                flux = frac * bulk(land_coef, ls)
                lf[:, here] = flux
            else:
                flux = (1.0 - frac) * bulk(ocean_coef, osv) + frac * bulk(ice_coef, isv)
                of[:, here] = flux
            next(sends).start()
            flux = flux.astype(jnp.bfloat16)
            fluxes += [flux[:, j * BL : (j + 1) * BL] for j in range(n)]
        for flux, pair, weight in zip(fluxes, slots, weights):
            terms = dot(flux, weight, NT).astype(send.dtype)
            for k in range(KR):
                send[pair[k]] = terms[:, k * BL : (k + 1) * BL]
    outs.append(pltpu.make_async_copy(send, send_hbm, out_sems.at[len(outs)]))
    outs[-1].start()
    for copy in outs:
        copy.wait()


def far(slots, got, near, os, ice, il, ls, ll, ot, lt):
    f32 = jnp.float32
    back = (got.shape[0], os.shape[0], BL)
    count = len(PARTS)
    return pl.pallas_call(
        far_kernel,
        out_shape=(
            jax.ShapeDtypeStruct(os.shape, f32),
            jax.ShapeDtypeStruct(ls.shape, f32),
            jax.ShapeDtypeStruct(back, jnp.bfloat16),
        ),
        in_specs=[whole(pl.ANY), *[whole()] * 7, *[whole(pl.ANY)] * 2],
        out_specs=[whole(pltpu.HBM)] * 3,
        scratch_shapes=[
            SMEM(slots.shape, slots.dtype),
            VMEM((ot.shape[0], KR, BL, BL), ot.dtype),
            VMEM((lt.shape[0], KR, BL, BL), lt.dtype),
            VMEM(os.shape, f32),
            VMEM(ls.shape, f32),
            VMEM(back, jnp.bfloat16),
            pltpu.SemaphoreType.DMA((count,)),
            pltpu.SemaphoreType.DMA((count + 1,)),
            pltpu.SemaphoreType.DMA(()),
        ],
        compiler_params=pltpu.CompilerParams(vmem_limit_bytes=50 << 20),
        name="far",
    )(slots, got, near, os, ice, il, ls, ll, ot, lt)


def near_back_kernel(ol_ref, ll_ref, of_ref, lf_ref, ot_ref, lt_ref, out_ref):
    step = pl.program_id(0)

    @pl.when(step == 0)
    def _():
        out_ref[...] = jnp.zeros(out_ref.shape, out_ref.dtype)

    for ids, flux, tiles in ((ol_ref, of_ref, ot_ref), (ll_ref, lf_ref, lt_ref)):
        n = tiles.shape[0]
        for b in range(n):
            g = flux[:, b * BL : (b + 1) * BL].astype(jnp.bfloat16)
            terms = dot(g, tiles[b].reshape(2 * BL, BL), NT)
            for k in range(2):
                at = lanes(ids[k, step * n + b])
                out_ref[:, at] = out_ref[:, at] + terms[:, k * BL : (k + 1) * BL]


def near_back(ol, ll, of, lf, ot, lt):
    ob, lb = ot.shape[0], lt.shape[0]
    ns = of.shape[0]
    return pl.pallas_call(
        near_back_kernel,
        grid=(STEPS,),
        out_shape=jax.ShapeDtypeStruct((ns, AB * BL), jnp.float32),
        in_specs=[
            whole(SMEM),
            whole(SMEM),
            pl.BlockSpec((ns, ob // STEPS * BL), lambda i: (0, i)),
            pl.BlockSpec((ns, lb // STEPS * BL), lambda i: (0, i)),
            *tile_specs(ob, lb, 1),
        ],
        out_specs=pl.BlockSpec((ns, AB * BL), lambda i: (0, 0)),
        compiler_params=pltpu.CompilerParams(vmem_limit_bytes=GRANT),
        cost_estimate=pl.CostEstimate(
            flops=2 * (ob + lb) * 2 * BL * BL * 128,
            bytes_accessed=(ob + lb) * 2 * BL * BL * 2,
            transcendentals=0,
        ),
        name="near_back",
    )(ol, ll, of, lf, ot, lt)


def collect_kernel(cells, neighbours, asked_hbm, back_ref, *refs):
    asked_ref, asked_sem, *refs = refs[-2:] + refs[:-2]
    ask = pltpu.make_async_copy(asked_hbm, asked_ref, asked_sem)
    ask.start()
    if neighbours:
        out_ref, *totals = refs
    else:
        acc_ref, out_ref, acc, sem, *totals = refs
        load = pltpu.make_async_copy(acc_ref, acc, sem)
        load.start()
        totals = [acc, *totals]
    cell = lax.axis_index("cell")
    half = cells // 2
    for total in totals[-CHAINS:]:
        total[...] = jnp.zeros(total.shape, jnp.float32)
    ask.wait()

    def body(c, _):
        far_one = jnp.logical_or(c <= cell - half, c > cell + half)

        @pl.when(far_one == neighbours)
        def _():
            for r in range(CAP):
                total = totals[r % CHAINS - CHAINS]
                first = asked_ref[c, r]
                at = first - AB * BL if neighbours else jnp.minimum(first, AB * BL)
                at = lanes_from(at)
                total[:, at] = total[:, at] + back_ref[c * CAP + r].astype(jnp.float32)

        return 0

    lax.fori_loop(0, cells, body, 0)
    if not neighbours:
        load.wait()
    for b in range(AB):
        here = slice(b * BL, (b + 1) * BL)
        total = functools.reduce(jnp.add, [ref[:, here] for ref in totals])
        out_ref[:, here] = total.astype(out_ref.dtype)


def collect(asked, back, acc, neighbours, cells):
    ns = back.shape[1]
    shape = (ns, AB * BL)
    accs, more = (), []
    if acc is not None:
        accs, more = (acc,), [VMEM(shape, jnp.float32), pltpu.SemaphoreType.DMA(())]
    return pl.pallas_call(
        functools.partial(collect_kernel, cells, neighbours),
        out_shape=jax.ShapeDtypeStruct(shape, jnp.float32 if accs else back.dtype),
        in_specs=[whole(pl.ANY), whole(), *[whole(pltpu.HBM)] * len(accs)],
        out_specs=whole(),
        scratch_shapes=[
            *more,
            *[VMEM((ns, (AB + 1) * BL), jnp.float32)] * CHAINS,
            SMEM(asked.shape, asked.dtype),
            pltpu.SemaphoreType.DMA(()),
        ],
        compiler_params=pltpu.CompilerParams(vmem_limit_bytes=SMALL),
        cost_estimate=pl.CostEstimate(
            flops=1 << 20, bytes_accessed=4 << 20, transcendentals=0
        ),
        name="collect_far" if neighbours else "collect_own",
    )(asked, back, *accs)


def per_device(
    sects, cells, atm_fields, ocn_state, ice_state, ice_level, lnd_state, lnd_level,
    ocn_map, ocn_local, ocn_tiles, lnd_map, lnd_local, lnd_tiles,
):
    axes = ("sect", "cell")
    count = sects * cells
    half = cells // 2
    to_server = []
    for q in range(count):
        s, c = divmod(q, cells)
        to_server.append((q, (s + (1 if c >= half else -1)) % sects * cells + c))
    to_owner = [(b, a) for a, b in to_server]
    exchange = functools.partial(
        lax.all_to_all, axis_name="cell", split_axis=0, concat_axis=0, tiled=True
    )

    near_fields = lax.ppermute(atm_fields, axes, to_server)
    asking, slots = requests(ocn_map.T, lnd_map.T, cells)
    asked = exchange(asking)
    held = hold(atm_fields, near_fields)
    got = exchange(serve(asked, held, cells))
    ol, ll = ocn_local.T, lnd_local.T
    near = near_mix(ol, ll, held, ocn_tiles, lnd_tiles)
    of, lf, send = far(
        slots, got, near, ocn_state, ice_state, ice_level.reshape(-1, BL), lnd_state,
        lnd_level.reshape(-1, BL), ocn_tiles, lnd_tiles,
    )
    back = exchange(send)
    acc = near_back(ol, ll, of, lf, ocn_tiles, lnd_tiles)
    back, acc = lax.optimization_barrier((back, acc))
    away = lax.ppermute(collect(asked, back, None, True, cells), axes, to_owner)
    own = collect(asked, back, acc, False, cells)
    return own + away.astype(jnp.float32), of, lf


def solution(mesh):
    a = ("sect", "cell")
    in_specs = (
        P(None, a), P(None, a), P(None, a), P(a), P(None, a), P(a),
        P(a, None), P(a, None), P(a, None, None, None),
        P(a, None), P(a, None), P(a, None, None, None),
    )
    return jax.shard_map(
        functools.partial(per_device, mesh.shape["sect"], mesh.shape["cell"]),
        mesh=mesh,
        in_specs=in_specs,
        out_specs=(P(None, a), P(None, a), P(None, a)),
        check_vma=False,
    )
```

```python
import functools

import jax
import jax.numpy as jnp
from jax import lax
from jax.experimental import pallas as pl
from jax.experimental.pallas import tpu as pltpu
from jax.sharding import PartitionSpec as P

ocean_coef = (1.2, 0.9, 1.5, 0.7, 1.1, 1.3, 0.8, 1.0)
ice_coef = (0.5, 1.4, 0.6, 1.2, 0.9, 0.4, 1.6, 0.7)
land_coef = (0.8, 1.1, 0.6, 1.5, 0.7, 1.2, 1.0, 0.5)

BL = 128
AB_BITS = 5
AB = 1 << AB_BITS
KR = KL = 2
CAP = 15
GRANT, LARGE, SMALL = 60 << 20, 50 << 20, 8 << 20
CHAINS = 5
VMEM = pltpu.VMEM
SMEM = pltpu.SMEM
NN = (((1,), (0,)), ((), ()))
NT = (((1,), (1,)), ((), ()))


def dot(a, b, dims):
    return lax.dot_general(a, b, dims, preferred_element_type=jnp.float32)


def lanes(i):
    return pl.ds(pl.multiple_of(i * BL, BL), BL)


def whole(space=VMEM):
    return pl.BlockSpec(memory_space=space)


def column(values, width):
    row = lax.broadcasted_iota(jnp.int32, (8, BL), 0)
    out = jnp.full((8, BL), values[7], jnp.float32)
    for j in range(7):
        out = jnp.where(row == j, values[j], out)
    return jnp.concatenate([out] * (width // BL), axis=1)


def request_kernel(cells, om_ref, lm_ref, req_ref, slot_ref):
    sect = lax.axis_index("sect")
    cell_bits = cells.bit_length() - 1
    before = jnp.zeros((cells, 1), jnp.float32)
    req = jnp.zeros((cells, BL), jnp.float32)
    slot_ref[...] = jnp.zeros(slot_ref.shape, jnp.int32)
    row = 0
    for ref in (om_ref, lm_ref):
        n = ref.shape[1]
        earlier = lax.broadcasted_iota(jnp.int32, (n, n), 0) < lax.broadcasted_iota(
            jnp.int32, (n, n), 1
        )
        earlier = jnp.where(earlier, 1.0, 0.0).astype(jnp.bfloat16)
        for k in range(ref.shape[0]):
            src = ref[k : k + 1, :]
            owner = src >> AB_BITS
            col = owner & (cells - 1)
            value = (src & (AB - 1)) + jnp.where(owner >> cell_bits == sect, 0, AB)
            chosen = lax.broadcasted_iota(jnp.int32, (cells, n), 0) == col
            onehot = jnp.where(chosen, 1.0, 0.0)
            ranks = before + dot(onehot.astype(jnp.bfloat16), earlier, NN)
            rank = jnp.sum(jnp.where(chosen, ranks, 0.0), axis=0, keepdims=True)
            before = before + jnp.sum(onehot, axis=1, keepdims=True)
            place = lax.broadcasted_iota(jnp.int32, (BL, n), 0) == rank.astype(jnp.int32)
            place = jnp.where(place, 1.0, 0.0).astype(jnp.bfloat16)
            asked = jnp.where(chosen, (value + 1).astype(jnp.float32), 0.0)
            req = req + dot(asked.astype(jnp.bfloat16), place, NT)
            slot_ref[row : row + 1, :n] = col * CAP + rank.astype(jnp.int32)
            row += 1
    req_ref[...] = req.astype(jnp.int32) - 1


def requests(om, lm, cells):
    return pl.pallas_call(
        functools.partial(request_kernel, cells),
        out_shape=(
            jax.ShapeDtypeStruct((cells, BL), jnp.int32),
            jax.ShapeDtypeStruct((8, BL), jnp.int32),
        ),
        in_specs=[whole()] * 2,
        out_specs=[whole()] * 2,
        compiler_params=pltpu.CompilerParams(vmem_limit_bytes=GRANT),
        name="requests",
    )(om, lm)


def hold_kernel(own_ref, near_ref, out_ref):
    nf, width = own_ref.shape
    rows = lax.broadcasted_iota(jnp.int32, (nf, nf), 0)
    pick = 3 * (rows & 7) + (rows >> 3) == lax.broadcasted_iota(jnp.int32, (nf, nf), 1)
    pick = jnp.where(pick, 1.0, 0.0).astype(own_ref.dtype)
    for k, ref in enumerate((own_ref, near_ref)):
        for at in range(0, width, 8 * BL):
            part = dot(pick, ref[:, at : at + 8 * BL], NN)
            out_ref[:, k * width + at : k * width + at + 8 * BL] = part.astype(out_ref.dtype)


def hold(own, near):
    return pl.pallas_call(
        hold_kernel,
        out_shape=jax.ShapeDtypeStruct((own.shape[0], 2 * own.shape[1]), own.dtype),
        in_specs=[whole()] * 2,
        out_specs=whole(),
        compiler_params=pltpu.CompilerParams(vmem_limit_bytes=SMALL),
        cost_estimate=pl.CostEstimate(flops=1 << 20, bytes_accessed=4 << 20, transcendentals=0),
        name="hold",
    )(own, near)


def serve_kernel(cells, asked_ref, both, out_ref, made, out_sems):
    def out(c):
        part = pl.ds(c * CAP, CAP)
        return pltpu.make_async_copy(made.at[part], out_ref.at[part], out_sems.at[c])

    def body(c, _):
        for r in range(CAP):
            i = jnp.maximum(asked_ref[c, r], 0)
            made[c * CAP + r] = both[:, lanes(i)]
        out(c).start()
        return 0

    lax.fori_loop(0, cells, body, 0)
    for c in range(cells):
        out(c).wait()


def serve(asked, both, cells):
    shape = (cells * CAP, both.shape[0], BL)
    return pl.pallas_call(
        functools.partial(serve_kernel, cells),
        out_shape=jax.ShapeDtypeStruct(shape, both.dtype),
        in_specs=[whole(SMEM), whole()],
        out_specs=whole(pltpu.HBM),
        scratch_shapes=[VMEM(shape, both.dtype), pltpu.SemaphoreType.DMA((cells,))],
        compiler_params=pltpu.CompilerParams(vmem_limit_bytes=SMALL),
        name="serve",
    )(asked, both)


STEPS = 4
PARTS = (0, 4, 10, 16)


def tile_specs(ob, lb, half):
    return [
        pl.BlockSpec((ob // STEPS, 2, BL, BL), lambda i: (i, half, 0, 0)),
        pl.BlockSpec((lb // STEPS, 2, BL, BL), lambda i: (i, half, 0, 0)),
    ]


def near_mix_kernel(ol_ref, ll_ref, f_ref, ot_ref, lt_ref, out_ref):
    step = pl.program_id(0)
    at = 0
    for ids, tiles in ((ol_ref, ot_ref), (ll_ref, lt_ref)):
        n = tiles.shape[0]
        for b in range(n):
            src = [f_ref[:, lanes(ids[k, step * n + b])] for k in range(2)]
            out_ref[at] = dot(
                jnp.concatenate(src, axis=1), tiles[b].reshape(2 * BL, BL), NN
            )
            at += 1


def near_mix(ol, ll, fields, ot, lt):
    ob, lb = ot.shape[0], lt.shape[0]
    nf = fields.shape[0]
    return pl.pallas_call(
        near_mix_kernel,
        grid=(STEPS,),
        out_shape=jax.ShapeDtypeStruct((ob + lb, nf, BL), jnp.float32),
        in_specs=[
            whole(SMEM),
            whole(SMEM),
            pl.BlockSpec(fields.shape, lambda i: (0, 0)),
            *tile_specs(ob, lb, 1),
        ],
        out_specs=pl.BlockSpec(((ob + lb) // STEPS, nf, BL), lambda i: (i, 0, 0)),
        compiler_params=pltpu.CompilerParams(vmem_limit_bytes=52 << 20),
        cost_estimate=pl.CostEstimate(
            flops=2 * (ob + lb) * 2 * BL * BL * 128,
            bytes_accessed=(ob + lb) * 2 * BL * BL * 2,
            transcendentals=0,
        ),
        name="near_mix",
    )(ol, ll, fields, ot, lt)


def portions(ob, lb):
    cuts = [ob * p // 16 for p in PARTS]
    out = [[(0, lo, hi)] for lo, hi in zip(cuts[:-1], cuts[1:])]
    out[-1].append((1, 0, lb))
    return out


def far_kernel(
    slot_hbm, got_ref, near, osv, isv, il, ls, ll, ot_hbm, lt_hbm, of_hbm, lf_hbm, send,
    slot_ref, ot, lt, of, lf, in_sems, out_sems, slot_sem,
):
    ob, lb = ot.shape[0], lt.shape[0]
    no, nl = ob // STEPS, lb // STEPS
    parts = portions(ob, lb)
    ins, outs = [], []
    for part in parts:
        for kind, lo, hi in part:
            hbm, on_chip = (lt_hbm, lt) if kind else (ot_hbm, ot)
            some = pl.ds(lo, hi - lo)
            copy = pltpu.make_async_copy(
                hbm.at[some, pl.ds(0, KR)], on_chip.at[some], in_sems.at[len(ins)]
            )
            copy.start()
            ins.append(copy)
            flux, flux_hbm = (lf, lf_hbm) if kind else (of, of_hbm)
            some = pl.ds(lo * BL, (hi - lo) * BL)
            outs.append(
                pltpu.make_async_copy(flux.at[:, some], flux_hbm.at[:, some], out_sems.at[len(outs)])
            )
        if part is parts[0]:
            load = pltpu.make_async_copy(slot_hbm, slot_ref, slot_sem)
            load.start()
    send[...] = jnp.zeros(send.shape, send.dtype)
    load.wait()
    waits, sends = iter(ins), iter(outs)
    for part in parts:
        for _ in part:
            next(waits).wait()
        work = [(kind, b) for kind, lo, hi in part for b in range(lo, hi)]
        slots = [[slot_ref[2 * kind + k, b] for k in range(KR)] for kind, b in work]
        weights = [(lt if kind else ot)[b].reshape(KR * BL, BL) for kind, b in work]
        rows = []
        for (kind, b), pair, weight in zip(work, slots, weights):
            at = (b // nl) * (no + nl) + no + b % nl if kind else (b // no) * (no + nl) + b % no
            source = jnp.concatenate([got_ref[s] for s in pair], axis=1)
            rows.append(near[at] + dot(source, weight, NN))
        fluxes = []
        for kind, lo, hi in part:
            n = hi - lo
            mine = rows[len(fluxes) : len(fluxes) + n]
            u, v, t = (
                jnp.concatenate([row[8 * j : 8 * j + 8] for row in mine], axis=1) for j in range(3)
            )
            wind = jnp.sqrt(1.0 + u * u + v * v)
            here = slice(lo * BL, hi * BL)
            level = (ll if kind else il)[lo:hi, :].astype(jnp.float32) * 0.125
            level = [jnp.broadcast_to(level[j : j + 1], (8, BL)) for j in range(n)]
            frac = jnp.concatenate(level, axis=1)

            def bulk(factors, state):
                return column(factors, n * BL) * wind * (t - state[:, here])

            if kind:
                flux = frac * bulk(land_coef, ls)
                lf[:, here] = flux
            else:
                flux = (1.0 - frac) * bulk(ocean_coef, osv) + frac * bulk(ice_coef, isv)
                of[:, here] = flux
            next(sends).start()
            flux = flux.astype(jnp.bfloat16)
            fluxes += [flux[:, j * BL : (j + 1) * BL] for j in range(n)]
        for flux, pair, weight in zip(fluxes, slots, weights):
            terms = dot(flux, weight, NT).astype(send.dtype)
            for k in range(KR):
                send[pair[k]] = terms[:, k * BL : (k + 1) * BL]
    for copy in outs:
        copy.wait()


def far(slots, got, near, os, ice, il, ls, ll, ot, lt):
    f32 = jnp.float32
    back = (got.shape[0], os.shape[0], BL)
    count = len(PARTS)
    return pl.pallas_call(
        far_kernel,
        out_shape=(
            jax.ShapeDtypeStruct(os.shape, f32),
            jax.ShapeDtypeStruct(ls.shape, f32),
            jax.ShapeDtypeStruct(back, jnp.bfloat16),
        ),
        in_specs=[whole(pl.ANY), *[whole()] * 7, *[whole(pl.ANY)] * 2],
        out_specs=[whole(pltpu.HBM), whole(pltpu.HBM), whole()],
        scratch_shapes=[
            SMEM(slots.shape, slots.dtype),
            VMEM((ot.shape[0], KR, BL, BL), ot.dtype),
            VMEM((lt.shape[0], KR, BL, BL), lt.dtype),
            VMEM(os.shape, f32),
            VMEM(ls.shape, f32),
            pltpu.SemaphoreType.DMA((count,)),
            pltpu.SemaphoreType.DMA((count + 1,)),
            pltpu.SemaphoreType.DMA(()),
        ],
        compiler_params=pltpu.CompilerParams(vmem_limit_bytes=50 << 20),
        name="far",
    )(slots, got, near, os, ice, il, ls, ll, ot, lt)


def near_back_kernel(ol_ref, ll_ref, of_ref, lf_ref, ot_hbm, lt_hbm, out_ref, ot, lt, sems):
    ob, lb = ot.shape[0], lt.shape[0]
    parts = portions(ob, lb)
    ins = []
    for i, part in enumerate(parts):
        for kind, lo, hi in part:
            hbm, on_chip = (lt_hbm, lt) if kind else (ot_hbm, ot)
            some = pl.ds(lo, hi - lo)
            copy = pltpu.make_async_copy(
                hbm.at[some, pl.ds(KR, KL)], on_chip.at[some], sems.at[len(ins)]
            )
            copy.start()
            ins.append(copy)
    out_ref[...] = jnp.zeros(out_ref.shape, out_ref.dtype)
    waits = iter(ins)
    for part in parts:
        for kind, lo, hi in part:
            next(waits).wait()
            ids, flux, tiles = (ll_ref, lf_ref, lt) if kind else (ol_ref, of_ref, ot)
            for b in range(lo, hi):
                g = flux[:, b * BL : (b + 1) * BL].astype(jnp.bfloat16)
                terms = dot(g, tiles[b].reshape(KL * BL, BL), NT)
                for k in range(KL):
                    to = lanes(ids[k, b])
                    out_ref[:, to] = out_ref[:, to] + terms[:, k * BL : (k + 1) * BL]


def near_back(ol, ll, of, lf, ot, lt):
    ob, lb = ot.shape[0], lt.shape[0]
    return pl.pallas_call(
        near_back_kernel,
        out_shape=jax.ShapeDtypeStruct((of.shape[0], AB * BL), jnp.float32),
        in_specs=[whole(SMEM), whole(SMEM), whole(), whole(), whole(pl.ANY), whole(pl.ANY)],
        out_specs=whole(),
        scratch_shapes=[
            VMEM((ob, KL, BL, BL), ot.dtype),
            VMEM((lb, KL, BL, BL), lt.dtype),
            pltpu.SemaphoreType.DMA((len(PARTS),)),
        ],
        compiler_params=pltpu.CompilerParams(vmem_limit_bytes=GRANT),
        cost_estimate=pl.CostEstimate(
            flops=2 * (ob + lb) * 2 * BL * BL * 128,
            bytes_accessed=(ob + lb) * 2 * BL * BL * 2,
            transcendentals=0,
        ),
        name="near_back",
    )(ol, ll, of, lf, ot, lt)


def collect_kernel(cells, neighbours, asked_hbm, back_ref, *refs):
    asked_ref, asked_sem, *refs = refs[-2:] + refs[:-2]
    ask = pltpu.make_async_copy(asked_hbm, asked_ref, asked_sem)
    ask.start()
    if neighbours:
        out_ref, *totals = refs
    else:
        acc_ref, out_ref, acc, sem, *totals = refs
        load = pltpu.make_async_copy(acc_ref, acc, sem)
        load.start()
        totals = [acc, *totals]
    cell = lax.axis_index("cell")
    half = cells // 2
    for total in totals[-CHAINS:]:
        total[...] = jnp.zeros(total.shape, jnp.float32)
    ask.wait()

    def body(c, _):
        far_one = jnp.logical_or(c <= cell - half, c > cell + half)

        @pl.when(far_one == neighbours)
        def _():
            for r in range(CAP):
                total = totals[r % CHAINS - CHAINS]
                i = asked_ref[c, r]
                at = lanes(jnp.where(i < 0, AB, i & (AB - 1)))
                total[:, at] = total[:, at] + back_ref[c * CAP + r].astype(jnp.float32)

        return 0

    lax.fori_loop(0, cells, body, 0)
    if not neighbours:
        load.wait()
    for b in range(AB):
        here = slice(b * BL, (b + 1) * BL)
        total = functools.reduce(jnp.add, [ref[:, here] for ref in totals])
        out_ref[:, here] = total.astype(out_ref.dtype)


def collect(asked, back, acc, neighbours, cells):
    ns = back.shape[1]
    shape = (ns, AB * BL)
    accs, more = (), []
    if acc is not None:
        accs, more = (acc,), [VMEM(shape, jnp.float32), pltpu.SemaphoreType.DMA(())]
    return pl.pallas_call(
        functools.partial(collect_kernel, cells, neighbours),
        out_shape=jax.ShapeDtypeStruct(shape, jnp.float32 if accs else back.dtype),
        in_specs=[whole(pl.ANY), whole(), *[whole(pltpu.HBM)] * len(accs)],
        out_specs=whole(),
        scratch_shapes=[
            *more,
            *[VMEM((ns, (AB + 1) * BL), jnp.float32)] * CHAINS,
            SMEM(asked.shape, asked.dtype),
            pltpu.SemaphoreType.DMA(()),
        ],
        compiler_params=pltpu.CompilerParams(vmem_limit_bytes=SMALL),
        cost_estimate=pl.CostEstimate(
            flops=1 << 20, bytes_accessed=4 << 20, transcendentals=0
        ),
        name="collect_far" if neighbours else "collect_own",
    )(asked, back, *accs)


def per_device(
    sects, cells, atm_fields, ocn_state, ice_state, ice_level, lnd_state, lnd_level,
    ocn_map, ocn_local, ocn_tiles, lnd_map, lnd_local, lnd_tiles,
):
    axes = ("sect", "cell")
    count = sects * cells
    half = cells // 2
    to_server = []
    for q in range(count):
        s, c = divmod(q, cells)
        to_server.append((q, (s + (1 if c >= half else -1)) % sects * cells + c))
    to_owner = [(b, a) for a, b in to_server]
    exchange = functools.partial(
        lax.all_to_all, axis_name="cell", split_axis=0, concat_axis=0, tiled=True
    )

    near_fields = lax.ppermute(atm_fields, axes, to_server)
    asking, slots = requests(ocn_map.T, lnd_map.T, cells)
    asked = exchange(asking)
    held = hold(atm_fields, near_fields)
    got = exchange(serve(asked, held, cells))
    ol, ll = ocn_local.T, lnd_local.T
    near = near_mix(ol, ll, held, ocn_tiles, lnd_tiles)
    of, lf, send = far(
        slots, got, near, ocn_state, ice_state, ice_level.reshape(-1, BL), lnd_state,
        lnd_level.reshape(-1, BL), ocn_tiles, lnd_tiles,
    )
    back = exchange(send)
    acc = near_back(ol, ll, of, lf, ocn_tiles, lnd_tiles)
    away = lax.ppermute(collect(asked, back, None, True, cells), axes, to_owner)
    own = collect(asked, back, acc, False, cells)
    return own + away.astype(jnp.float32), of, lf


def solution(mesh):
    a = ("sect", "cell")
    in_specs = (
        P(None, a), P(None, a), P(None, a), P(a), P(None, a), P(a),
        P(a, None), P(a, None), P(a, None, None, None),
        P(a, None), P(a, None), P(a, None, None, None),
    )
    return jax.shard_map(
        functools.partial(per_device, mesh.shape["sect"], mesh.shape["cell"]),
        mesh=mesh,
        in_specs=in_specs,
        out_specs=(P(None, a), P(None, a), P(None, a)),
        check_vma=False,
    )
```

```python
import functools

import jax
import jax.numpy as jnp
from jax import lax
from jax.experimental import pallas as pl
from jax.experimental.pallas import tpu as pltpu
from jax.sharding import PartitionSpec as P

ocean_coef = (1.2, 0.9, 1.5, 0.7, 1.1, 1.3, 0.8, 1.0)
ice_coef = (0.5, 1.4, 0.6, 1.2, 0.9, 0.4, 1.6, 0.7)
land_coef = (0.8, 1.1, 0.6, 1.5, 0.7, 1.2, 1.0, 0.5)

BL = 128
AB_BITS = 5
AB = 1 << AB_BITS
KR = KL = 2
CAP = 15
GRANT, LARGE, SMALL = 60 << 20, 50 << 20, 8 << 20
CHAINS = 3
VMEM = pltpu.VMEM
SMEM = pltpu.SMEM
NN = (((1,), (0,)), ((), ()))
NT = (((1,), (1,)), ((), ()))


def dot(a, b, dims):
    return lax.dot_general(a, b, dims, preferred_element_type=jnp.float32)


def lanes(i):
    return pl.ds(pl.multiple_of(i * BL, BL), BL)


def lanes_from(first):
    return pl.ds(pl.multiple_of(first, BL), BL)


def whole(space=VMEM):
    return pl.BlockSpec(memory_space=space)


def column(values, width):
    row = lax.broadcasted_iota(jnp.int32, (8, BL), 0)
    out = jnp.full((8, BL), values[7], jnp.float32)
    for j in range(7):
        out = jnp.where(row == j, values[j], out)
    return jnp.concatenate([out] * (width // BL), axis=1)


def request_kernel(cells, om_ref, lm_ref, req_ref, slot_ref):
    sect = lax.axis_index("sect")
    cell_bits = cells.bit_length() - 1
    before = jnp.zeros((cells, 1), jnp.float32)
    req = jnp.zeros((cells, BL), jnp.float32)
    slot_ref[...] = jnp.zeros(slot_ref.shape, jnp.int32)
    row = 0
    for ref in (om_ref, lm_ref):
        n = ref.shape[1]
        earlier = lax.broadcasted_iota(jnp.int32, (n, n), 0) < lax.broadcasted_iota(
            jnp.int32, (n, n), 1
        )
        earlier = jnp.where(earlier, 1.0, 0.0).astype(jnp.bfloat16)
        for k in range(ref.shape[0]):
            src = ref[k : k + 1, :]
            owner = src >> AB_BITS
            col = owner & (cells - 1)
            value = (src & (AB - 1)) + jnp.where(owner >> cell_bits == sect, 0, AB)
            chosen = lax.broadcasted_iota(jnp.int32, (cells, n), 0) == col
            onehot = jnp.where(chosen, 1.0, 0.0)
            ranks = before + dot(onehot.astype(jnp.bfloat16), earlier, NN)
            rank = jnp.sum(jnp.where(chosen, ranks, 0.0), axis=0, keepdims=True)
            before = before + jnp.sum(onehot, axis=1, keepdims=True)
            place = lax.broadcasted_iota(jnp.int32, (BL, n), 0) == rank.astype(jnp.int32)
            place = jnp.where(place, 1.0, 0.0).astype(jnp.bfloat16)
            asked = jnp.where(chosen, (value + 1).astype(jnp.float32), 0.0)
            req = req + dot(asked.astype(jnp.bfloat16), place, NT)
            slot_ref[row : row + 1, :n] = col * CAP + rank.astype(jnp.int32)
            row += 1
    asked = req.astype(jnp.int32)
    req_ref[...] = jnp.where(asked == 0, 2 * AB, asked - 1) * BL


def requests(om, lm, cells):
    return pl.pallas_call(
        functools.partial(request_kernel, cells),
        out_shape=(
            jax.ShapeDtypeStruct((cells, BL), jnp.int32),
            jax.ShapeDtypeStruct((8, BL), jnp.int32),
        ),
        in_specs=[whole()] * 2,
        out_specs=[whole()] * 2,
        compiler_params=pltpu.CompilerParams(vmem_limit_bytes=GRANT),
        name="requests",
    )(om, lm)


def hold_kernel(own_ref, near_ref, out_ref):
    nf, width = own_ref.shape
    rows = lax.broadcasted_iota(jnp.int32, (nf, nf), 0)
    pick = 3 * (rows & 7) + (rows >> 3) == lax.broadcasted_iota(jnp.int32, (nf, nf), 1)
    pick = jnp.where(pick, 1.0, 0.0).astype(own_ref.dtype)
    for k, ref in enumerate((own_ref, near_ref)):
        for at in range(0, width, 8 * BL):
            part = dot(pick, ref[:, at : at + 8 * BL], NN)
            out_ref[:, k * width + at : k * width + at + 8 * BL] = part.astype(out_ref.dtype)
    out_ref[:, 2 * width :] = jnp.zeros((nf, BL), out_ref.dtype)


def hold(own, near):
    return pl.pallas_call(
        hold_kernel,
        out_shape=jax.ShapeDtypeStruct((own.shape[0], 2 * own.shape[1] + BL), own.dtype),
        in_specs=[whole()] * 2,
        out_specs=whole(),
        compiler_params=pltpu.CompilerParams(vmem_limit_bytes=SMALL),
        cost_estimate=pl.CostEstimate(flops=1 << 20, bytes_accessed=4 << 20, transcendentals=0),
        name="hold",
    )(own, near)


def serve_kernel(cells, asked_ref, both, out_ref, made, out_sems):
    def out(c):
        part = pl.ds(c * CAP, CAP)
        return pltpu.make_async_copy(made.at[part], out_ref.at[part], out_sems.at[c])

    def body(c, _):
        for r in range(CAP):
            made[c * CAP + r] = both[:, lanes_from(asked_ref[c, r])]
        out(c).start()
        return 0

    lax.fori_loop(0, cells, body, 0)
    for c in range(cells):
        out(c).wait()


def serve(asked, both, cells):
    shape = (cells * CAP, both.shape[0], BL)
    return pl.pallas_call(
        functools.partial(serve_kernel, cells),
        out_shape=jax.ShapeDtypeStruct(shape, both.dtype),
        in_specs=[whole(SMEM), whole()],
        out_specs=whole(pltpu.HBM),
        scratch_shapes=[VMEM(shape, both.dtype), pltpu.SemaphoreType.DMA((cells,))],
        compiler_params=pltpu.CompilerParams(vmem_limit_bytes=SMALL),
        name="serve",
    )(asked, both)


STEPS = 4
PARTS = (0, 4, 10, 16)


def tile_specs(ob, lb, half):
    return [
        pl.BlockSpec((ob // STEPS, 2, BL, BL), lambda i: (i, half, 0, 0)),
        pl.BlockSpec((lb // STEPS, 2, BL, BL), lambda i: (i, half, 0, 0)),
    ]


def near_mix_kernel(ol_ref, ll_ref, f_ref, ot_ref, lt_ref, out_ref):
    step = pl.program_id(0)
    at = 0
    for ids, tiles in ((ol_ref, ot_ref), (ll_ref, lt_ref)):
        n = tiles.shape[0]
        for b in range(n):
            src = [f_ref[:, lanes(ids[k, step * n + b])] for k in range(2)]
            out_ref[at] = dot(
                jnp.concatenate(src, axis=1), tiles[b].reshape(2 * BL, BL), NN
            )
            at += 1


def near_mix(ol, ll, fields, ot, lt):
    ob, lb = ot.shape[0], lt.shape[0]
    nf = fields.shape[0]
    return pl.pallas_call(
        near_mix_kernel,
        grid=(STEPS,),
        out_shape=jax.ShapeDtypeStruct((ob + lb, nf, BL), jnp.float32),
        in_specs=[
            whole(SMEM),
            whole(SMEM),
            pl.BlockSpec(fields.shape, lambda i: (0, 0)),
            *tile_specs(ob, lb, 1),
        ],
        out_specs=pl.BlockSpec(((ob + lb) // STEPS, nf, BL), lambda i: (i, 0, 0)),
        compiler_params=pltpu.CompilerParams(vmem_limit_bytes=52 << 20),
        cost_estimate=pl.CostEstimate(
            flops=2 * (ob + lb) * 2 * BL * BL * 128,
            bytes_accessed=(ob + lb) * 2 * BL * BL * 2,
            transcendentals=0,
        ),
        name="near_mix",
    )(ol, ll, fields, ot, lt)


def portions(ob, lb):
    cuts = [ob * p // 16 for p in PARTS]
    out = [[(0, lo, hi)] for lo, hi in zip(cuts[:-1], cuts[1:])]
    out[-1].append((1, 0, lb))
    return out


def far_kernel(
    slot_hbm, got_ref, near, osv, isv, il, ls, ll, ot_hbm, lt_hbm, of_hbm, lf_hbm, send_hbm,
    slot_ref, ot, lt, of, lf, send, in_sems, out_sems, slot_sem,
):
    ob, lb = ot.shape[0], lt.shape[0]
    no, nl = ob // STEPS, lb // STEPS
    parts = portions(ob, lb)
    ins, outs = [], []
    for part in parts:
        for kind, lo, hi in part:
            hbm, on_chip = (lt_hbm, lt) if kind else (ot_hbm, ot)
            some = pl.ds(lo, hi - lo)
            copy = pltpu.make_async_copy(
                hbm.at[some, pl.ds(0, KR)], on_chip.at[some], in_sems.at[len(ins)]
            )
            copy.start()
            ins.append(copy)
            flux, flux_hbm = (lf, lf_hbm) if kind else (of, of_hbm)
            some = pl.ds(lo * BL, (hi - lo) * BL)
            outs.append(
                pltpu.make_async_copy(flux.at[:, some], flux_hbm.at[:, some], out_sems.at[len(outs)])
            )
        if part is parts[0]:
            load = pltpu.make_async_copy(slot_hbm, slot_ref, slot_sem)
            load.start()
    send[...] = jnp.zeros(send.shape, send.dtype)
    load.wait()
    waits, sends = iter(ins), iter(outs)
    for part in parts:
        for _ in part:
            next(waits).wait()
        work = [(kind, b) for kind, lo, hi in part for b in range(lo, hi)]
        slots = [[slot_ref[2 * kind + k, b] for k in range(KR)] for kind, b in work]
        weights = [(lt if kind else ot)[b].reshape(KR * BL, BL) for kind, b in work]
        rows = []
        for (kind, b), pair, weight in zip(work, slots, weights):
            at = (b // nl) * (no + nl) + no + b % nl if kind else (b // no) * (no + nl) + b % no
            source = jnp.concatenate([got_ref[s] for s in pair], axis=1)
            rows.append(near[at] + dot(source, weight, NN))
        fluxes = []
        for kind, lo, hi in part:
            n = hi - lo
            mine = rows[len(fluxes) : len(fluxes) + n]
            u, v, t = (
                jnp.concatenate([row[8 * j : 8 * j + 8] for row in mine], axis=1) for j in range(3)
            )
            wind = jnp.sqrt(1.0 + u * u + v * v)
            here = slice(lo * BL, hi * BL)
            level = (ll if kind else il)[lo:hi, :].astype(jnp.float32) * 0.125
            level = [jnp.broadcast_to(level[j : j + 1], (8, BL)) for j in range(n)]
            frac = jnp.concatenate(level, axis=1)

            def bulk(factors, state):
                return column(factors, n * BL) * wind * (t - state[:, here])

            if kind:
                flux = frac * bulk(land_coef, ls)
                lf[:, here] = flux
            else:
                flux = (1.0 - frac) * bulk(ocean_coef, osv) + frac * bulk(ice_coef, isv)
                of[:, here] = flux
            next(sends).start()
            flux = flux.astype(jnp.bfloat16)
            fluxes += [flux[:, j * BL : (j + 1) * BL] for j in range(n)]
        for flux, pair, weight in zip(fluxes, slots, weights):
            terms = dot(flux, weight, NT).astype(send.dtype)
            for k in range(KR):
                send[pair[k]] = terms[:, k * BL : (k + 1) * BL]
    outs.append(pltpu.make_async_copy(send, send_hbm, out_sems.at[len(outs)]))
    outs[-1].start()
    for copy in outs:
        copy.wait()


def far(slots, got, near, os, ice, il, ls, ll, ot, lt):
    f32 = jnp.float32
    back = (got.shape[0], os.shape[0], BL)
    count = len(PARTS)
    return pl.pallas_call(
        far_kernel,
        out_shape=(
            jax.ShapeDtypeStruct(os.shape, f32),
            jax.ShapeDtypeStruct(ls.shape, f32),
            jax.ShapeDtypeStruct(back, jnp.bfloat16),
        ),
        in_specs=[whole(pl.ANY), *[whole()] * 7, *[whole(pl.ANY)] * 2],
        out_specs=[whole(pltpu.HBM)] * 3,
        scratch_shapes=[
            SMEM(slots.shape, slots.dtype),
            VMEM((ot.shape[0], KR, BL, BL), ot.dtype),
            VMEM((lt.shape[0], KR, BL, BL), lt.dtype),
            VMEM(os.shape, f32),
            VMEM(ls.shape, f32),
            VMEM(back, jnp.bfloat16),
            pltpu.SemaphoreType.DMA((count,)),
            pltpu.SemaphoreType.DMA((count + 1,)),
            pltpu.SemaphoreType.DMA(()),
        ],
        compiler_params=pltpu.CompilerParams(vmem_limit_bytes=50 << 20),
        name="far",
    )(slots, got, near, os, ice, il, ls, ll, ot, lt)


def near_back_kernel(ol_ref, ll_ref, of_ref, lf_ref, ot_ref, lt_ref, out_ref):
    step = pl.program_id(0)

    @pl.when(step == 0)
    def _():
        out_ref[...] = jnp.zeros(out_ref.shape, out_ref.dtype)

    for ids, flux, tiles in ((ol_ref, of_ref, ot_ref), (ll_ref, lf_ref, lt_ref)):
        n = tiles.shape[0]
        for b in range(n):
            g = flux[:, b * BL : (b + 1) * BL].astype(jnp.bfloat16)
            terms = dot(g, tiles[b].reshape(2 * BL, BL), NT)
            for k in range(2):
                at = lanes(ids[k, step * n + b])
                out_ref[:, at] = out_ref[:, at] + terms[:, k * BL : (k + 1) * BL]


def near_back(ol, ll, of, lf, ot, lt):
    ob, lb = ot.shape[0], lt.shape[0]
    ns = of.shape[0]
    return pl.pallas_call(
        near_back_kernel,
        grid=(STEPS,),
        out_shape=jax.ShapeDtypeStruct((ns, AB * BL), jnp.float32),
        in_specs=[
            whole(SMEM),
            whole(SMEM),
            pl.BlockSpec((ns, ob // STEPS * BL), lambda i: (0, i)),
            pl.BlockSpec((ns, lb // STEPS * BL), lambda i: (0, i)),
            *tile_specs(ob, lb, 1),
        ],
        out_specs=pl.BlockSpec((ns, AB * BL), lambda i: (0, 0)),
        compiler_params=pltpu.CompilerParams(vmem_limit_bytes=GRANT),
        cost_estimate=pl.CostEstimate(
            flops=2 * (ob + lb) * 2 * BL * BL * 128,
            bytes_accessed=(ob + lb) * 2 * BL * BL * 2,
            transcendentals=0,
        ),
        name="near_back",
    )(ol, ll, of, lf, ot, lt)


def collect_kernel(cells, neighbours, asked_hbm, back_ref, *refs):
    asked_ref, asked_sem, *refs = refs[-2:] + refs[:-2]
    ask = pltpu.make_async_copy(asked_hbm, asked_ref, asked_sem)
    ask.start()
    if neighbours:
        out_ref, *totals = refs
    else:
        acc_ref, out_ref, acc, sem, *totals = refs
        load = pltpu.make_async_copy(acc_ref, acc, sem)
        load.start()
        totals = [acc, *totals]
    cell = lax.axis_index("cell")
    half = cells // 2
    for total in totals[-CHAINS:]:
        total[...] = jnp.zeros(total.shape, jnp.float32)
    ask.wait()

    def body(c, _):
        far_one = jnp.logical_or(c <= cell - half, c > cell + half)

        @pl.when(far_one == neighbours)
        def _():
            for r in range(CAP):
                total = totals[r % CHAINS - CHAINS]
                first = asked_ref[c, r]
                at = first - AB * BL if neighbours else jnp.minimum(first, AB * BL)
                at = lanes_from(at)
                total[:, at] = total[:, at] + back_ref[c * CAP + r].astype(jnp.float32)

        return 0

    lax.fori_loop(0, cells, body, 0)
    if not neighbours:
        load.wait()
    for b in range(AB):
        here = slice(b * BL, (b + 1) * BL)
        total = functools.reduce(jnp.add, [ref[:, here] for ref in totals])
        out_ref[:, here] = total.astype(out_ref.dtype)


def collect(asked, back, acc, neighbours, cells):
    ns = back.shape[1]
    shape = (ns, AB * BL)
    accs, more = (), []
    if acc is not None:
        accs, more = (acc,), [VMEM(shape, jnp.float32), pltpu.SemaphoreType.DMA(())]
    return pl.pallas_call(
        functools.partial(collect_kernel, cells, neighbours),
        out_shape=jax.ShapeDtypeStruct(shape, jnp.float32 if accs else back.dtype),
        in_specs=[whole(pl.ANY), whole(), *[whole(pltpu.HBM)] * len(accs)],
        out_specs=whole(),
        scratch_shapes=[
            *more,
            *[VMEM((ns, (AB + 1) * BL), jnp.float32)] * CHAINS,
            SMEM(asked.shape, asked.dtype),
            pltpu.SemaphoreType.DMA(()),
        ],
        compiler_params=pltpu.CompilerParams(vmem_limit_bytes=SMALL),
        cost_estimate=pl.CostEstimate(
            flops=1 << 20, bytes_accessed=4 << 20, transcendentals=0
        ),
        name="collect_far" if neighbours else "collect_own",
    )(asked, back, *accs)


def per_device(
    sects, cells, atm_fields, ocn_state, ice_state, ice_level, lnd_state, lnd_level,
    ocn_map, ocn_local, ocn_tiles, lnd_map, lnd_local, lnd_tiles,
):
    axes = ("sect", "cell")
    count = sects * cells
    half = cells // 2
    to_server = []
    for q in range(count):
        s, c = divmod(q, cells)
        to_server.append((q, (s + (1 if c >= half else -1)) % sects * cells + c))
    to_owner = [(b, a) for a, b in to_server]
    exchange = functools.partial(
        lax.all_to_all, axis_name="cell", split_axis=0, concat_axis=0, tiled=True
    )

    near_fields = lax.ppermute(atm_fields, axes, to_server)
    asking, slots = requests(ocn_map.T, lnd_map.T, cells)
    asked = exchange(asking)
    held = hold(atm_fields, near_fields)
    got = exchange(serve(asked, held, cells))
    ol, ll = ocn_local.T, lnd_local.T
    near = near_mix(ol, ll, held, ocn_tiles, lnd_tiles)
    of, lf, send = far(
        slots, got, near, ocn_state, ice_state, ice_level.reshape(-1, BL), lnd_state,
        lnd_level.reshape(-1, BL), ocn_tiles, lnd_tiles,
    )
    back = exchange(send)
    acc = near_back(ol, ll, of, lf, ocn_tiles, lnd_tiles)
    back, acc = lax.optimization_barrier((back, acc))
    away = lax.ppermute(collect(asked, back, None, True, cells), axes, to_owner)
    own = collect(asked, back, acc, False, cells)
    return own + away.astype(jnp.float32), of, lf


def solution(mesh):
    a = ("sect", "cell")
    in_specs = (
        P(None, a), P(None, a), P(None, a), P(a), P(None, a), P(a),
        P(a, None), P(a, None), P(a, None, None, None),
        P(a, None), P(a, None), P(a, None, None, None),
    )
    return jax.shard_map(
        functools.partial(per_device, mesh.shape["sect"], mesh.shape["cell"]),
        mesh=mesh,
        in_specs=in_specs,
        out_specs=(P(None, a), P(None, a), P(None, a)),
        check_vma=False,
    )
```
